1024 devices in a mesh: expert: 16 (over y_lo, z), dp: 64 (over y_hi, x, core).
Axes of the slice: x: 8, y: 8 (y_hi: 4, y_lo: 2; y = y_hi * 2 + y_lo), z: 8, core: 2. Of those that a mesh axis runs over, the one named last changes fastest.
Arguments:
- tokens: bfloat16 [8192, 4096], P('dp'), may hold values from -6 to 6
- first_expert: int32 [8192], P('dp'), may hold values from 0 to 1, as said below
- first_slot: int32 [8192], P('dp'), may hold values from -1 to 3, as said below
- second_expert: int32 [8192], P('dp'), may hold values from 0 to 1, as said below
- second_slot: int32 [8192], P('dp'), may hold values from -1 to 1, as said below
- first_gate: float32 [8192], P('dp'), may hold values from 0.3 to 1
- second_gate: float32 [8192], P('dp'), may hold values from 0.3 to 1
- w_gate: bfloat16 [8192, 16384], P('expert', 'dp'), may hold values from -0.09375 to 0.09375
- w_up: bfloat16 [8192, 16384], P('expert', 'dp'), may hold values from -0.09375 to 0.09375
- w_down: bfloat16 [16384, 8192], P('dp', 'expert'), may hold values from -0.046875 to 0.046875
- norm_gain: float32 [4096], replicated, may hold values from 0.25 to 1.75
- w_query: bfloat16 [4096, 8192], P('dp', 'expert'), may hold values from -0.09375 to 0.09375
Outputs:
- mixed: bfloat16 [8192, 4096], P('dp')
- query: bfloat16 [8192, 8192], P('dp', 'expert')
The draws below stay inside these ranges and needn't reach their ends.
Inputs may be any that keep to these rules, and one draw needn't show every extreme that they name: `first_expert`: in every dp row each expert is the first expert of exactly 64 tokens. `first_slot`: in every dp row and for every expert, the slots 0 to 3 are each taken by exactly one token of that expert; the rest of its tokens have -1. second_expert = 1 - first_expert for every token. `second_slot`: only tokens with first_slot = -1 have a second slot; in every dp row and for every expert, the slots 0 to 1 are each taken by exactly one token.
All inputs are finite; a program needn't handle non-finite values.
Results may differ from the reference program's by a relative error of at most 0.0051.
Values may be sent and summed in bfloat16 or wider, within the bound.
No kernel may reach another device: no remote copies, remote signals or barrier semaphores. Data moves between devices by JAX's collectives and lax.ppermute only.
A program may use at most 32 MiB of HBM per device.

```python
import jax
import jax.numpy as jnp
from jax import lax

D = 4096
QC = 8192
CAP1 = 4
CAP2 = 2
TOK_DEV = 128
EXPERTS = 2
HIDDEN_SIZE = 16384
TOKENS = 8192
N_DP = 64


def routing_table(key):
    row_tokens = TOK_DEV
    row_keys = jax.random.split(key, N_DP)
    rank_table = jax.vmap(lambda row_key: jax.random.permutation(row_key, row_tokens))(row_keys).astype(jnp.int32)
    shifts = jax.random.randint(jax.random.fold_in(key, 99), (N_DP, 1), 1, max(EXPERTS, 2)).astype(jnp.int32)
    first_ids = rank_table % EXPERTS
    expert_rank = rank_table // EXPERTS
    first_slots = jnp.where(expert_rank < CAP1, expert_rank, -1)
    second_ids = (first_ids + shifts) % EXPERTS
    second_slots = jnp.where((expert_rank >= CAP1) & (expert_rank < CAP1 + CAP2), expert_rank - CAP1, -1)
    return (first_ids.reshape(-1).astype(jnp.int32), first_slots.reshape(-1).astype(jnp.int32), second_ids.reshape(-1).astype(jnp.int32), second_slots.reshape(-1).astype(jnp.int32))


def draw_first_expert(key, part):
    return routing_table(key)[0]


def draw_first_slot(key, part):
    return routing_table(key)[1]


def draw_second_expert(key, part):
    return routing_table(key)[2]


def draw_second_slot(key, part):
    return routing_table(key)[3]


def levels(own_key, extent, cuts, smallest, high):
    gain, own = 1.0, jax.random.fold_in(own_key, 6)
    for dim, blocks in cuts:
        draws = jnp.exp(jax.random.uniform(jax.random.fold_in(own, dim), (blocks,), jnp.float32, smallest / len(cuts), high / len(cuts)))
        gain = gain * jnp.repeat(draws, extent[dim] // blocks).reshape([-1 if axis == dim else 1 for axis in range(len(extent))])
    return gain


def gaussian(key, shape, scale, bound, cuts=(), held_as=jnp.bfloat16):
    factor_of = levels(key, shape, cuts, -0.22, 0.18) if cuts else 1.0
    drawn = jax.random.normal(key, shape, jnp.float32) * scale * factor_of
    return jnp.minimum(jnp.maximum(drawn, -bound), bound).astype(held_as)


def setup_inputs(seed: int = 0) -> dict:
    keys = jax.random.split(jax.random.key(seed), 13)
    return {
        "tokens": gaussian(keys[0], (TOKENS, D), 1.0, 6.0, ((0, 64),)),
        "first_expert": draw_first_expert(jax.random.fold_in(keys[12], 71), 0),
        "first_slot": draw_first_slot(jax.random.fold_in(keys[12], 71), 0),
        "second_expert": draw_second_expert(jax.random.fold_in(keys[12], 71), 0),
        "second_slot": draw_second_slot(jax.random.fold_in(keys[12], 71), 0),
        "first_gate": jnp.clip(0.3 + 0.7 * jax.random.uniform(keys[5], (TOKENS,), jnp.float32) ** levels(keys[5], (TOKENS,), ((0, 64),), -0.2, 0.2), 0.3, 1.0),
        "second_gate": jnp.clip(0.3 + 0.7 * jax.random.uniform(keys[6], (TOKENS,), jnp.float32) ** levels(keys[6], (TOKENS,), ((0, 64),), -0.2, 0.2), 0.3, 1.0),
        "w_gate": gaussian(keys[7], (EXPERTS * D, HIDDEN_SIZE), D ** -0.5, 0.09375, ((0, 16), (1, 64))),
        "w_up": gaussian(keys[8], (EXPERTS * D, HIDDEN_SIZE), D ** -0.5, 0.09375, ((0, 16), (1, 64))),
        "w_down": gaussian(keys[9], (HIDDEN_SIZE, EXPERTS * D), HIDDEN_SIZE ** -0.5, 0.046875, ((0, 64), (1, 16))),
        "norm_gain": jnp.clip(1.0 + 0.15 * jax.random.normal(keys[10], (D,), jnp.float32), 0.25, 1.75),
        "w_query": gaussian(keys[11], (D, QC), D ** -0.5, 0.09375, ((0, 64), (1, 16))),
    }


def run_experts(table, w_gate, w_up, w_down):

    def one_expert(expert_index):
        expert_rows = lax.dynamic_index_in_dim(table, expert_index, 0, keepdims=False)
        first_row = (expert_index * D).astype(jnp.int32)
        gate_slice = lax.dynamic_slice_in_dim(w_gate, first_row, D, 0)
        up_slice = lax.dynamic_slice_in_dim(w_up, first_row, D, 0)
        down_slice = lax.dynamic_slice_in_dim(w_down, first_row, D, 1)
        gate = jnp.dot(expert_rows, gate_slice, preferred_element_type=jnp.float32)
        up_value = jnp.dot(expert_rows, up_slice, preferred_element_type=jnp.float32)
        hidden = (jax.nn.silu(gate) * up_value).astype(jnp.bfloat16)
        return jnp.dot(hidden, down_slice, preferred_element_type=jnp.float32).astype(jnp.bfloat16)
    return lax.map(one_expert, jnp.arange(EXPERTS, dtype=jnp.int32))

def one_round(tokens, expert_ids, slot_ids, capacity, w_gate, w_up, w_down):
    row_index = jnp.arange(TOKENS, dtype=jnp.int32) // TOK_DEV
    served = slot_ids >= 0
    total_rows = EXPERTS * N_DP * capacity
    position = jnp.where(served, expert_ids * (N_DP * capacity) + row_index * capacity + slot_ids, total_rows).astype(jnp.int32)
    table = jnp.zeros((total_rows + 1, D), jnp.bfloat16).at[position].set(tokens)
    table = table[:total_rows].reshape(EXPERTS, N_DP * capacity, D)
    outputs = run_experts(table, w_gate, w_up, w_down).reshape(total_rows, D)
    picked = outputs[jnp.where(served, position, 0).astype(jnp.int32)].astype(jnp.float32)
    return picked * served[:, None].astype(jnp.float32)

def reference(tokens, first_expert, first_slot, second_expert, second_slot, first_gate, second_gate, w_gate, w_up, w_down, norm_gain, w_query):
    first_out = one_round(tokens, first_expert, first_slot, CAP1, w_gate, w_up, w_down)
    second_out = one_round(tokens, second_expert, second_slot, CAP2, w_gate, w_up, w_down)
    mixed_float = tokens.astype(jnp.float32) + first_gate[:, None] * first_out + second_gate[:, None] * second_out
    mixed = mixed_float.astype(jnp.bfloat16)
    values = mixed.astype(jnp.float32)
    scale = lax.rsqrt(lax.optimization_barrier(jnp.mean(values * values, axis=-1, keepdims=True)) + 1e-05)
    normed = (values * scale * norm_gain[None, :]).astype(jnp.bfloat16)
    query = jnp.dot(normed, w_query, preferred_element_type=jnp.float32).astype(jnp.bfloat16)
    return (mixed, query)
```

```python
import jax
import jax.numpy as jnp
from jax import lax
from jax.sharding import Mesh, PartitionSpec as P

CAP1 = 4
CAP2 = 2
SLOTS = CAP1 + CAP2
EXPERT = ("y_lo", "z")
CHIPS = ("y_hi", "x")
DP = ("y_hi", "x", "core")
SIZES = {"y_lo": 2, "z": 8, "y_hi": 4, "x": 8, "core": 2}


def exchange(blocks, axes):
    return lax.all_to_all(blocks, axes, split_axis=0, concat_axis=0, tiled=True)


def spread(block, axes):
    count = lax.axis_size(axes)
    return exchange(jnp.broadcast_to(block[None], (count,) + block.shape), axes)


def other_core(block):
    return lax.ppermute(block, "core", [(0, 1), (1, 0)])


def local(
    tokens,
    first_expert,
    first_slot,
    second_expert,
    second_slot,
    first_gate,
    second_gate,
    w_gate,
    w_up,
    w_down,
    norm_gain,
    w_query,
):
    tok_count, width = tokens.shape
    blocks = lax.axis_size("z")
    experts = lax.axis_size("y_lo")
    chips = lax.axis_size(CHIPS)
    block_width = width // blocks
    units = w_gate.shape[1]
    own_expert = lax.axis_index("y_lo")
    own_block = lax.axis_index("z")

    w_query_full = lax.all_gather(w_query, DP, axis=0, tiled=True)
    w_gate_other = other_core(w_gate)
    w_up_other = other_core(w_up)
    w_down_other = other_core(w_down)

    served_first = first_slot >= 0
    served = served_first | (second_slot >= 0)
    expert_of = jnp.where(served_first, first_expert, second_expert)
    slot_of = jnp.where(served_first, first_slot, second_slot + CAP1)
    gate_of = jnp.where(served_first, first_gate, second_gate)

    token_block = lax.dynamic_slice_in_dim(tokens, own_block * block_width, block_width, 1)
    placement = jnp.where(served & (expert_of == own_expert), slot_of, -1)
    slot_hot = (jnp.arange(SLOTS, dtype=jnp.int32)[:, None] == placement[None, :]).astype(jnp.bfloat16)
    slot_rows = jnp.dot(slot_hot, token_block, preferred_element_type=jnp.float32).astype(jnp.bfloat16)

    rows = spread(slot_rows, CHIPS).reshape(chips * SLOTS, block_width)
    partial = jnp.concatenate(
        [
            jnp.dot(rows, w, preferred_element_type=jnp.float32).astype(jnp.bfloat16)
            for w in (w_gate, w_gate_other, w_up, w_up_other)
        ],
        axis=1,
    )
    share = chips * SLOTS // blocks
    summed = jnp.sum(
        exchange(partial.reshape(blocks, share, 4 * units), "z").astype(jnp.float32), axis=0
    )
    hidden_share = (jax.nn.silu(summed[:, : 2 * units]) * summed[:, 2 * units :]).astype(jnp.bfloat16)
    hidden = spread(hidden_share, "z").reshape(chips * SLOTS, 2 * units)
    out_part = jnp.dot(hidden[:, :units], w_down, preferred_element_type=jnp.float32) + jnp.dot(
        hidden[:, units:], w_down_other, preferred_element_type=jnp.float32
    )
    pieces = exchange(out_part.astype(jnp.bfloat16).reshape(chips, SLOTS, block_width), CHIPS)
    expert_out = jnp.sum(pieces.astype(jnp.float32), axis=0).astype(jnp.bfloat16)
    gathered = spread(expert_out, EXPERT).reshape(experts, blocks, SLOTS, block_width)
    expert_table = jnp.transpose(gathered, (0, 2, 1, 3)).reshape(experts * SLOTS, width)

    column = jnp.where(served, expert_of * SLOTS + slot_of, -1)
    pick_hot = (column[:, None] == jnp.arange(experts * SLOTS, dtype=jnp.int32)[None, :]).astype(jnp.bfloat16)
    picked = jnp.dot(pick_hot, expert_table, preferred_element_type=jnp.float32)
    mixed = (tokens.astype(jnp.float32) + gate_of[:, None] * picked).astype(jnp.bfloat16)
    values = mixed.astype(jnp.float32)
    scale = lax.rsqrt(jnp.mean(values * values, axis=-1, keepdims=True) + 1e-05)
    normed = (values * scale * norm_gain[None, :]).astype(jnp.bfloat16)
    query = jnp.dot(normed, w_query_full, preferred_element_type=jnp.float32).astype(jnp.bfloat16)
    return (mixed, query)


def solution(mesh):
    fine = Mesh(mesh.devices.reshape(tuple(SIZES.values())), tuple(SIZES))
    in_specs = (
        P(DP, None),
        P(DP),
        P(DP),
        P(DP),
        P(DP),
        P(DP),
        P(DP),
        P(EXPERT, DP),
        P(EXPERT, DP),
        P(DP, EXPERT),
        P(),
        P(DP, EXPERT),
    )
    out_specs = (P(DP, None), P(DP, EXPERT))
    return jax.shard_map(local, mesh=fine, in_specs=in_specs, out_specs=out_specs, check_vma=False)
```

```python
import jax
import jax.numpy as jnp
from jax import lax
from jax.experimental import pallas as pl
from jax.experimental.pallas import tpu as pltpu
from jax.sharding import Mesh, PartitionSpec as P

CAP1 = 4
CAP2 = 2
SLOTS = CAP1 + CAP2
EXPERT = ("y_lo", "z")
CHIPS = ("y_hi", "x")
DP = ("y_hi", "x", "core")
SIZES = {"y_lo": 2, "z": 8, "y_hi": 4, "x": 8, "core": 2}
PADDED = 8
LANES = 128


def exchange(blocks, axes):
    return lax.all_to_all(blocks, axes, split_axis=0, concat_axis=0, tiled=True)


def spread(block, axes):
    count = lax.axis_size(axes)
    return exchange(jnp.broadcast_to(block[None], (count,) + block.shape), axes)


def other_core(block):
    return lax.ppermute(block, "core", [(0, 1), (1, 0)])


def from_above(block, distance):
    count = lax.axis_size("y_hi")
    return lax.ppermute(block, "y_hi", [((i + distance) % count, i) for i in range(count)])


def outward(block, distance):
    count = lax.axis_size("x")
    route = []
    for i in range(count):
        route.append((2 * i, 2 * ((i + distance) % count)))
        route.append((2 * i + 1, 2 * ((i - distance) % count) + 1))
    return lax.ppermute(block, ("x", "core"), route)


def tie(*values):
    return lax.optimization_barrier(values)


def finish_kernel(
    place_ref, tokens_ref, table_ref, column_ref, gate_ref, gain_ref, *refs
):
    w_refs, (mixed_ref, query_ref, normed_ref) = refs[:-3], refs[-3:]
    x, y, core = place_ref[0], place_ref[1], place_ref[2]
    blocks = table_ref.shape[0] // (2 * PADDED)
    tok_count, width = tokens_ref.shape
    block_width = width // blocks
    column = column_ref[...]
    slots = lax.broadcasted_iota(jnp.int32, (tok_count, PADDED), 1)
    hot = [
        (column == slots + e * PADDED).astype(jnp.bfloat16) for e in range(2)
    ]
    gate = gate_ref[...]
    square = jnp.zeros((tok_count, LANES), jnp.float32)
    for z in range(blocks):
        cols = pl.ds(z * block_width, block_width)
        picked = sum(
            jnp.dot(
                hot[e],
                table_ref[pl.ds((e * blocks + z) * PADDED, PADDED), :],
                preferred_element_type=jnp.float32,
            )
            for e in range(2)
        )
        mixed = (tokens_ref[:, cols].astype(jnp.float32) + gate * picked).astype(jnp.bfloat16)
        mixed_ref[:, cols] = mixed
        values = mixed.astype(jnp.float32)
        for i in range(block_width // LANES):
            part = values[:, i * LANES : (i + 1) * LANES]
            square += part * part
    mean = jnp.sum(square, axis=1, keepdims=True) * (1.0 / width)
    scale = lax.rsqrt(mean + 1e-05)
    for z in range(blocks):
        cols = pl.ds(z * block_width, block_width)
        values = mixed_ref[:, cols].astype(jnp.float32)
        normed_ref[:, cols] = (values * scale * gain_ref[:, cols]).astype(jnp.bfloat16)
    sign = 1 - 2 * core
    xs = [0, -1, -2, -3, 4, 1, 2, 3, 4]
    query = jnp.zeros(query_ref.shape, jnp.float32)
    for w_ref, offset in zip(w_refs, xs, strict=True):
        far = abs(offset) == 4
        chip_x = lax.rem(x + sign * offset + 8, 8)
        if far:
            half = core if w_ref is w_refs[4] else 1 - core
        for j in range(w_ref.shape[0]):
            rel = j + half * 2 if far else j
            chip_y = lax.rem(y + rel, 4)
            start = pl.multiple_of((chip_y * 8 + chip_x) * LANES, LANES)
            query += jnp.dot(
                normed_ref[:, pl.ds(start, LANES)], w_ref[j], preferred_element_type=jnp.float32
            )
    query_ref[...] = query.astype(query_ref.dtype)


def finish(place, tokens, table, column, gate, gain, weights):
    vmem = pl.BlockSpec(memory_space=pltpu.VMEM)
    tok_count, width = tokens.shape
    columns = weights[0].shape[-1]
    return pl.pallas_call(
        finish_kernel,
        out_shape=(
            jax.ShapeDtypeStruct((tok_count, width), jnp.bfloat16),
            jax.ShapeDtypeStruct((tok_count, columns), jnp.bfloat16),
        ),
        in_specs=[pl.BlockSpec(memory_space=pltpu.SMEM)] + [vmem] * (5 + len(weights)),
        out_specs=(vmem, vmem),
        scratch_shapes=[pltpu.VMEM((tok_count, width), jnp.bfloat16)],
        compiler_params=pltpu.CompilerParams(vmem_limit_bytes=24 * 1024 * 1024),
        cost_estimate=pl.CostEstimate(
            flops=2 * tok_count * width * columns, bytes_accessed=4 * width * columns, transcendentals=0
        ),
    )(place, tokens, table, column[:, None], gate[:, None], gain[None, :], *weights)


def local(
    tokens,
    first_expert,
    first_slot,
    second_expert,
    second_slot,
    first_gate,
    second_gate,
    w_gate,
    w_up,
    w_down,
    norm_gain,
    w_query,
):
    tok_count, width = tokens.shape
    blocks = lax.axis_size("z")
    chips = lax.axis_size(CHIPS)
    block_width = width // blocks
    units = w_gate.shape[1]
    own_expert = lax.axis_index("y_lo")
    own_block = lax.axis_index("z")
    core = lax.axis_index("core")

    served_first = first_slot >= 0
    served = served_first | (second_slot >= 0)
    expert_of = jnp.where(served_first, first_expert, second_expert)
    slot_of = jnp.where(served_first, first_slot, second_slot + CAP1)
    gate_of = jnp.where(served_first, first_gate, second_gate)

    token_block = lax.dynamic_slice_in_dim(tokens, own_block * block_width, block_width, 1)
    placement = jnp.where(served & (expert_of == own_expert), slot_of, -1)
    slot_hot = (jnp.arange(SLOTS, dtype=jnp.int32)[:, None] == placement[None, :]).astype(jnp.bfloat16)
    slot_rows = jnp.dot(slot_hot, token_block, preferred_element_type=jnp.float32).astype(jnp.bfloat16)

    chip_rows = other_core(w_query)
    chip_rows = jnp.where(
        core == 0, jnp.concatenate([w_query, chip_rows], 0), jnp.concatenate([chip_rows, w_query], 0)
    )
    slot_rows, chip_rows = tie(slot_rows, chip_rows)
    rows = spread(slot_rows, CHIPS).reshape(chips * SLOTS, block_width)
    w_gate_other = other_core(w_gate)
    w_up_other = other_core(w_up)
    query_own = jnp.stack([chip_rows] + [from_above(chip_rows, i) for i in (1, 2, 3)])

    partial = jnp.concatenate(
        [
            jnp.dot(rows, w, preferred_element_type=jnp.float32).astype(jnp.bfloat16)
            for w in (w_gate, w_gate_other, w_up, w_up_other)
        ],
        axis=1,
    )
    share = chips * SLOTS // blocks
    partial, query_own = tie(partial, query_own)
    summed = exchange(partial.reshape(blocks, share, 4 * units), "z")
    near = [outward(query_own, 1), outward(query_own, 2)]
    summed = jnp.sum(summed.astype(jnp.float32), axis=0)
    hidden_share = (jax.nn.silu(summed[:, : 2 * units]) * summed[:, 2 * units :]).astype(jnp.bfloat16)
    hidden_share, near[0], near[1] = tie(hidden_share, *near)
    hidden = spread(hidden_share, "z").reshape(chips * SLOTS, 2 * units)
    w_down_other = other_core(w_down)
    far_half = lax.dynamic_slice_in_dim(near[1], 2 * core, 2, 0)
    far = [outward(near[0], 2), outward(far_half, 2)]
    out_part = jnp.dot(hidden[:, :units], w_down, preferred_element_type=jnp.float32) + jnp.dot(
        hidden[:, units:], w_down_other, preferred_element_type=jnp.float32
    )
    out_part = out_part.astype(jnp.bfloat16)
    pieces = exchange(out_part.reshape(chips, SLOTS, block_width), CHIPS)
    expert_out = jnp.sum(pieces.astype(jnp.float32), axis=0).astype(jnp.bfloat16)
    expert_out = jnp.concatenate([expert_out, jnp.zeros((PADDED - SLOTS, block_width), jnp.bfloat16)], 0)
    expert_out, far[0], far[1] = tie(expert_out, *far)
    table = spread(expert_out, EXPERT).reshape(-1, block_width)
    arrived = near + far
    weights = [query_own] + arrived + [other_core(block) for block in arrived]

    column = jnp.where(served, expert_of * PADDED + slot_of, -1)
    place = jnp.stack([lax.axis_index("x"), lax.axis_index("y_hi"), core]).astype(jnp.int32)
    return finish(place, tokens, table, column, gate_of, norm_gain, weights)


def solution(mesh):
    fine = Mesh(mesh.devices.reshape(tuple(SIZES.values())), tuple(SIZES))
    in_specs = (
        P(DP, None),
        P(DP),
        P(DP),
        P(DP),
        P(DP),
        P(DP),
        P(DP),
        P(EXPERT, DP),
        P(EXPERT, DP),
        P(DP, EXPERT),
        P(),
        P(DP, EXPERT),
    )
    out_specs = (P(DP, None), P(DP, EXPERT))
    return jax.shard_map(local, mesh=fine, in_specs=in_specs, out_specs=out_specs, check_vma=False)
```

```python
import jax
import jax.numpy as jnp
from jax import lax
from jax.experimental import pallas as pl
from jax.experimental.pallas import tpu as pltpu
from jax.sharding import Mesh, PartitionSpec as P

CAP1 = 4
CAP2 = 2
SLOTS = CAP1 + CAP2
EXPERT = ("y_lo", "z")
CHIPS = ("y_hi", "x")
DP = ("y_hi", "x", "core")
SIZES = {"y_lo": 2, "z": 8, "y_hi": 4, "x": 8, "core": 2}
PADDED = 8
LANES = 128


def exchange(blocks, axes):
    return lax.all_to_all(blocks, axes, split_axis=0, concat_axis=0, tiled=True)


def spread(block, axes):
    count = lax.axis_size(axes)
    return exchange(jnp.broadcast_to(block[None], (count,) + block.shape), axes)


def other_core(block):
    return lax.ppermute(block, "core", [(0, 1), (1, 0)])


def pack(rows):
    lead, (count, width) = rows.shape[:-2], rows.shape[-2:]
    rows = jnp.pad(rows, [(0, 0)] * len(lead) + [(0, PADDED - count), (0, 0)])
    rows = jnp.moveaxis(rows.reshape(lead + (PADDED, width // LANES, LANES)), -2, -3)
    return rows.reshape(lead + (PADDED * width // LANES, LANES))


def finish_kernel(
    core_ref, tokens_ref, table_ref, column_ref, gate_ref, gain_ref, a_ref, b_ref, a_other_ref, b_other_ref,
    mixed_ref, query_ref, normed_ref,
):
    core = core_ref[0]
    experts = 2
    blocks = table_ref.shape[0] // experts
    packed = table_ref.shape[1]
    groups = packed // PADDED
    tok_count, width = tokens_ref.shape
    block_width = width // blocks
    column = column_ref[...]
    slots = lax.broadcasted_iota(jnp.int32, (tok_count, PADDED), 1)
    hot = [(column == slots + e * PADDED).astype(jnp.bfloat16) for e in range(experts)]
    gate = gate_ref[...]
    square = jnp.zeros((tok_count, LANES), jnp.float32)
    for z in range(blocks):
        cols = pl.ds(z * block_width, block_width)
        picked = jnp.zeros((tok_count, block_width), jnp.float32)
        for e in range(experts):
            rows = [table_ref[e * blocks + z, pl.ds(g * PADDED, PADDED), :] for g in range(groups)]
            picked += jnp.dot(hot[e], jnp.concatenate(rows, axis=1), preferred_element_type=jnp.float32)
        mixed = (tokens_ref[:, cols].astype(jnp.float32) + gate * picked).astype(jnp.bfloat16)
        mixed_ref[:, cols] = mixed
        values = mixed.astype(jnp.float32)
        for i in range(block_width // LANES):
            part = values[:, i * LANES : (i + 1) * LANES]
            square += part * part
    mean = jnp.sum(square, axis=1, keepdims=True) * (1.0 / width)
    scale = lax.rsqrt(mean + 1e-05)
    for z in range(blocks):
        cols = pl.ds(z * block_width, block_width)
        values = mixed_ref[:, cols].astype(jnp.float32)
        normed_ref[:, cols] = (values * scale * gain_ref[:, cols]).astype(jnp.bfloat16)

    def product(w_ref):
        w = w_ref[:, pl.ds(packed, w_ref.shape[1] - packed), :].reshape(width, LANES)
        return jnp.dot(normed_ref[...], w, preferred_element_type=jnp.float32)

    own = jnp.concatenate([product(a_ref), product(b_ref)], axis=1).astype(query_ref.dtype)
    other = jnp.concatenate([product(a_other_ref), product(b_other_ref)], axis=1).astype(query_ref.dtype)
    half = own.shape[1]
    query_ref[:, pl.ds(0, half)] = jnp.where(core == 0, own, other)
    query_ref[:, pl.ds(half, half)] = jnp.where(core == 0, other, own)


def finish(core, tokens, table, column, gate, gain, weights):
    vmem = pl.BlockSpec(memory_space=pltpu.VMEM)
    tok_count, width = tokens.shape
    columns = len(weights) * LANES
    return pl.pallas_call(
        finish_kernel,
        out_shape=(
            jax.ShapeDtypeStruct((tok_count, width), jnp.bfloat16),
            jax.ShapeDtypeStruct((tok_count, columns), jnp.bfloat16),
        ),
        in_specs=[pl.BlockSpec(memory_space=pltpu.SMEM)] + [vmem] * (5 + len(weights)),
        out_specs=(vmem, vmem),
        scratch_shapes=[pltpu.VMEM((tok_count, width), jnp.bfloat16)],
        compiler_params=pltpu.CompilerParams(vmem_limit_bytes=24 * 1024 * 1024),
        cost_estimate=pl.CostEstimate(
            flops=2 * tok_count * width * columns, bytes_accessed=4 * width * columns, transcendentals=0
        ),
    )(core[None], tokens, table, column[:, None], gate[:, None], gain[None, :], *weights)


def local(
    tokens,
    first_expert,
    first_slot,
    second_expert,
    second_slot,
    first_gate,
    second_gate,
    w_gate,
    w_up,
    w_down,
    norm_gain,
    w_query,
):
    tok_count, width = tokens.shape
    blocks = lax.axis_size("z")
    chips = lax.axis_size(CHIPS)
    block_width = width // blocks
    units = w_gate.shape[1]
    own_expert = lax.axis_index("y_lo")
    own_block = lax.axis_index("z")
    core = lax.axis_index("core")

    served_first = first_slot >= 0
    served = served_first | (second_slot >= 0)
    expert_of = jnp.where(served_first, first_expert, second_expert)
    slot_of = jnp.where(served_first, first_slot, second_slot + CAP1)
    gate_of = jnp.where(served_first, first_gate, second_gate)

    token_block = lax.dynamic_slice_in_dim(tokens, own_block * block_width, block_width, 1)
    placement = jnp.where(served & (expert_of == own_expert), slot_of, -1)
    slot_hot = (jnp.arange(SLOTS, dtype=jnp.int32)[:, None] == placement[None, :]).astype(jnp.bfloat16)
    slot_rows = jnp.dot(slot_hot, token_block, preferred_element_type=jnp.float32).astype(jnp.bfloat16)

    half = w_query.shape[1] // 2
    own_cols = lax.dynamic_slice_in_dim(w_query, core * half, half, 1)
    came = other_core(lax.dynamic_slice_in_dim(w_query, (1 - core) * half, half, 1))
    pair = jnp.where(core == 0, jnp.concatenate([own_cols, came], 0), jnp.concatenate([came, own_cols], 0))
    w_a, w_b = pair[:, :LANES], pair[:, LANES:]

    packed = PADDED * block_width // LANES
    query_a = spread(jnp.concatenate([pack(slot_rows), w_a], 0), CHIPS)
    w_gate_other = other_core(w_gate)
    w_up_other = other_core(w_up)
    query_a_other = other_core(query_a)
    rows = query_a[:, :packed].reshape(chips, -1, PADDED, LANES)[:, :, :SLOTS]
    rows = jnp.moveaxis(rows, 1, 2).reshape(chips * SLOTS, block_width)

    partial = jnp.concatenate(
        [
            jnp.dot(rows, w, preferred_element_type=jnp.float32).astype(jnp.bfloat16)
            for w in (w_gate, w_gate_other, w_up, w_up_other)
        ],
        axis=1,
    )
    share = chips * SLOTS // blocks
    summed = exchange(partial.reshape(blocks, share, 4 * units), "z")
    summed = jnp.sum(summed.astype(jnp.float32), axis=0)
    hidden_share = (jax.nn.silu(summed[:, : 2 * units]) * summed[:, 2 * units :]).astype(jnp.bfloat16)
    hidden = spread(hidden_share, "z").reshape(chips * SLOTS, 2 * units)
    w_down_other = other_core(w_down)
    out_part = jnp.dot(hidden[:, :units], w_down, preferred_element_type=jnp.float32) + jnp.dot(
        hidden[:, units:], w_down_other, preferred_element_type=jnp.float32
    )
    out_part = pack(out_part.astype(jnp.bfloat16).reshape(chips, SLOTS, block_width))
    query_b = exchange(
        jnp.concatenate([out_part, jnp.broadcast_to(w_b[None], (chips,) + w_b.shape)], 1), CHIPS
    )
    query_b_other = other_core(query_b)
    expert_out = jnp.sum(query_b[:, :packed].astype(jnp.float32), axis=0).astype(jnp.bfloat16)
    table = spread(expert_out, EXPERT)

    column = jnp.where(served, expert_of * PADDED + slot_of, -1)
    return finish(
        core, tokens, table, column, gate_of, norm_gain, [query_a, query_b, query_a_other, query_b_other]
    )


def solution(mesh):
    fine = Mesh(mesh.devices.reshape(tuple(SIZES.values())), tuple(SIZES))
    in_specs = (
        P(DP, None),
        P(DP),
        P(DP),
        P(DP),
        P(DP),
        P(DP),
        P(DP),
        P(EXPERT, DP),
        P(EXPERT, DP),
        P(DP, EXPERT),
        P(),
        P(DP, EXPERT),
    )
    out_specs = (P(DP, None), P(DP, EXPERT))
    return jax.shard_map(local, mesh=fine, in_specs=in_specs, out_specs=out_specs, check_vma=False)
```

```python
import jax
import jax.numpy as jnp
from jax import lax
from jax.experimental import pallas as pl
from jax.experimental.pallas import tpu as pltpu
from jax.sharding import Mesh, PartitionSpec as P

CAP1 = 4
CAP2 = 2
SLOTS = CAP1 + CAP2
EXPERT = ("y_lo", "z")
CHIPS = ("y_hi", "x")
DP = ("y_hi", "x", "core")
SIZES = {"y_lo": 2, "z": 8, "y_hi": 4, "x": 8, "core": 2}
PADDED = 8
LANES = 128
Y_OFFSETS = (0, -1, 1, 2)


def exchange(blocks, axes):
    return lax.all_to_all(blocks, axes, split_axis=0, concat_axis=0, tiled=True)


def copies(block, axes):
    return jnp.broadcast_to(block[None], (lax.axis_size(axes),) + block.shape)


def other_core(block):
    return lax.ppermute(block, "core", [(0, 1), (1, 0)])


def along(axis, block, distance):
    count = lax.axis_size(axis)
    return lax.ppermute(block, axis, [(i, (i + distance) % count) for i in range(count)])


def tie(*values):
    return lax.optimization_barrier(values)


def finish_kernel(
    place_ref, tokens_ref, table_ref, column_ref, gate_ref, gain_ref, *refs
):
    w_refs, (mixed_ref, query_ref, normed_ref) = refs[:-3], refs[-3:]
    x, y, core = place_ref[0], place_ref[1], place_ref[2]
    blocks = table_ref.shape[0] // (2 * PADDED)
    tok_count, width = tokens_ref.shape
    block_width = width // blocks
    column = column_ref[...]
    slots = lax.broadcasted_iota(jnp.int32, (tok_count, PADDED), 1)
    hot = [
        (column == slots + e * PADDED).astype(jnp.bfloat16) for e in range(2)
    ]
    gate = gate_ref[...]
    square = jnp.zeros((tok_count, LANES), jnp.float32)
    for z in range(blocks):
        cols = pl.ds(z * block_width, block_width)
        picked = sum(
            jnp.dot(
                hot[e],
                table_ref[pl.ds((e * blocks + z) * PADDED, PADDED), :],
                preferred_element_type=jnp.float32,
            )
            for e in range(2)
        )
        mixed = (tokens_ref[:, cols].astype(jnp.float32) + gate * picked).astype(jnp.bfloat16)
        mixed_ref[:, cols] = mixed
        values = mixed.astype(jnp.float32)
        for i in range(block_width // LANES):
            part = values[:, i * LANES : (i + 1) * LANES]
            square += part * part
    mean = jnp.sum(square, axis=1, keepdims=True) * (1.0 / width)
    scale = lax.rsqrt(mean + 1e-05)
    for z in range(blocks):
        cols = pl.ds(z * block_width, block_width)
        values = mixed_ref[:, cols].astype(jnp.float32)
        normed_ref[:, cols] = (values * scale * gain_ref[:, cols]).astype(jnp.bfloat16)

    def product(low_refs, high_refs):
        query = jnp.zeros(query_ref.shape, jnp.float32)
        for low, high, base, count in zip(low_refs, high_refs, (x, x - 1, x + 1), (3, 3, 2), strict=True):
            for j, y_offset in enumerate(Y_OFFSETS):
                for i in range(count):
                    chip_x = lax.rem(base + 3 * (i - 1) + 8, 8)
                    chip_y = lax.rem(y + y_offset + 4, 4)
                    start = pl.multiple_of((chip_y * 8 + chip_x) * LANES, LANES)
                    block = jnp.concatenate([low[j, i], high[j, i]], axis=0)
                    query += jnp.dot(
                        normed_ref[:, pl.ds(start, LANES)], block, preferred_element_type=jnp.float32
                    )
        query_ref[...] = query.astype(query_ref.dtype)

    own, other = w_refs[:3], w_refs[3:]

    @pl.when(core == 0)
    def _():
        product(own, other)

    @pl.when(core != 0)
    def _():
        product(other, own)


def finish(place, tokens, table, column, gate, gain, weights):
    vmem = pl.BlockSpec(memory_space=pltpu.VMEM)
    tok_count, width = tokens.shape
    columns = weights[0].shape[-1]
    return pl.pallas_call(
        finish_kernel,
        out_shape=(
            jax.ShapeDtypeStruct((tok_count, width), jnp.bfloat16),
            jax.ShapeDtypeStruct((tok_count, columns), jnp.bfloat16),
        ),
        in_specs=[pl.BlockSpec(memory_space=pltpu.SMEM)] + [vmem] * (5 + len(weights)),
        out_specs=(vmem, vmem),
        scratch_shapes=[pltpu.VMEM((tok_count, width), jnp.bfloat16)],
        compiler_params=pltpu.CompilerParams(vmem_limit_bytes=24 * 1024 * 1024),
        cost_estimate=pl.CostEstimate(
            flops=2 * tok_count * width * columns, bytes_accessed=4 * width * columns, transcendentals=0
        ),
    )(place, tokens, table, column[:, None], gate[:, None], gain[None, :], *weights)


def local(
    tokens,
    first_expert,
    first_slot,
    second_expert,
    second_slot,
    first_gate,
    second_gate,
    w_gate,
    w_up,
    w_down,
    norm_gain,
    w_query,
):
    tok_count, width = tokens.shape
    blocks = lax.axis_size("z")
    chips = lax.axis_size(CHIPS)
    block_width = width // blocks
    units = w_gate.shape[1]
    own_expert = lax.axis_index("y_lo")
    own_block = lax.axis_index("z")
    core = lax.axis_index("core")

    served_first = first_slot >= 0
    served = served_first | (second_slot >= 0)
    expert_of = jnp.where(served_first, first_expert, second_expert)
    slot_of = jnp.where(served_first, first_slot, second_slot + CAP1)
    gate_of = jnp.where(served_first, first_gate, second_gate)

    token_block = lax.dynamic_slice_in_dim(tokens, own_block * block_width, block_width, 1)
    placement = jnp.where(served & (expert_of == own_expert), slot_of, -1)
    slot_hot = (jnp.arange(SLOTS, dtype=jnp.int32)[:, None] == placement[None, :]).astype(jnp.bfloat16)
    slot_rows = jnp.dot(slot_hot, token_block, preferred_element_type=jnp.float32).astype(jnp.bfloat16)

    slot_copies, w_query = tie(copies(slot_rows, CHIPS), w_query)
    rows = exchange(slot_copies, CHIPS).reshape(chips * SLOTS, block_width)
    w_gate_other = other_core(w_gate)
    w_up_other = other_core(w_up)
    chip_set = jnp.stack([along("x", w_query, 3), w_query, along("x", w_query, -3)])

    partial = jnp.concatenate(
        [
            jnp.dot(rows, w, preferred_element_type=jnp.float32).astype(jnp.bfloat16)
            for w in (w_gate, w_gate_other, w_up, w_up_other)
        ],
        axis=1,
    )
    share = chips * SLOTS // blocks
    partial, chip_set = tie(partial, chip_set)
    summed = exchange(partial.reshape(blocks, share, 4 * units), "z")
    beside = [along("y_hi", chip_set, -offset) for offset in Y_OFFSETS[1:]]
    summed = jnp.sum(summed.astype(jnp.float32), axis=0)
    hidden_share = (jax.nn.silu(summed[:, : 2 * units]) * summed[:, 2 * units :]).astype(jnp.bfloat16)
    hidden_copies, *beside = tie(copies(hidden_share, "z"), *beside)
    hidden = exchange(hidden_copies, "z").reshape(chips * SLOTS, 2 * units)
    w_down_other = other_core(w_down)
    column_set = jnp.stack([chip_set] + beside)
    below, above = along("x", column_set, 1), along("x", column_set, -1)
    out_part = jnp.dot(hidden[:, :units], w_down, preferred_element_type=jnp.float32) + jnp.dot(
        hidden[:, units:], w_down_other, preferred_element_type=jnp.float32
    )
    out_part = out_part.astype(jnp.bfloat16)
    pieces = exchange(out_part.reshape(chips, SLOTS, block_width), CHIPS)
    expert_out = jnp.sum(pieces.astype(jnp.float32), axis=0).astype(jnp.bfloat16)
    expert_out = jnp.concatenate([expert_out, jnp.zeros((PADDED - SLOTS, block_width), jnp.bfloat16)], 0)
    out_copies, below, above = tie(copies(expert_out, EXPERT), below, above)
    table = exchange(out_copies, EXPERT).reshape(-1, block_width)
    weights = [column_set, below, above]
    weights += [other_core(w) for w in weights]

    column = jnp.where(served, expert_of * PADDED + slot_of, -1)
    place = jnp.stack([lax.axis_index("x"), lax.axis_index("y_hi"), core]).astype(jnp.int32)
    return finish(place, tokens, table, column, gate_of, norm_gain, weights)


def solution(mesh):
    fine = Mesh(mesh.devices.reshape(tuple(SIZES.values())), tuple(SIZES))
    in_specs = (
        P(DP, None),
        P(DP),
        P(DP),
        P(DP),
        P(DP),
        P(DP),
        P(DP),
        P(EXPERT, DP),
        P(EXPERT, DP),
        P(DP, EXPERT),
        P(),
        P(DP, EXPERT),
    )
    out_specs = (P(DP, None), P(DP, EXPERT))
    return jax.shard_map(local, mesh=fine, in_specs=in_specs, out_specs=out_specs, check_vma=False)
```

```python
import jax
import jax.numpy as jnp
from jax import lax
from jax.experimental import pallas as pl
from jax.experimental.pallas import tpu as pltpu
from jax.sharding import Mesh, PartitionSpec as P

CAP1 = 4
CAP2 = 2
SLOTS = CAP1 + CAP2
EXPERT = ("y_lo", "z")
CHIPS = ("y_hi", "x")
DP = ("y_hi", "x", "core")
SIZES = {"y_lo": 2, "z": 8, "y_hi": 4, "x": 8, "core": 2}
PADDED = 8
LANES = 128


def exchange(blocks, axes):
    return lax.all_to_all(blocks, axes, split_axis=0, concat_axis=0, tiled=True)


def copies(block, axes):
    return jnp.broadcast_to(block[None], (lax.axis_size(axes),) + block.shape)


def other_core(block):
    return lax.ppermute(block, "core", [(0, 1), (1, 0)])


def along(axis, block, distance):
    count = lax.axis_size(axis)
    return lax.ppermute(block, axis, [(i, (i + distance) % count) for i in range(count)])


def tie(*values):
    return lax.optimization_barrier(values)


def finish_kernel(
    tokens_ref, table_ref, column_ref, gate_ref, gain_ref, w_hbm, mixed_ref, query_ref, normed_ref, w_ref, sem
):
    parts = w_ref.shape[0]
    loads = [pltpu.make_async_copy(w_hbm.at[i], w_ref.at[i], sem.at[i]) for i in range(parts)]
    for load in loads:
        load.start()
    blocks = table_ref.shape[0] // (2 * PADDED)
    tok_count, width = tokens_ref.shape
    block_width = width // blocks
    column = column_ref[...]
    slots = lax.broadcasted_iota(jnp.int32, (tok_count, PADDED), 1)
    hot = [(column == slots + e * PADDED).astype(jnp.bfloat16) for e in range(2)]
    gate = gate_ref[...]
    square = jnp.zeros((tok_count, LANES), jnp.float32)
    for z in range(blocks):
        cols = pl.ds(z * block_width, block_width)
        picked = sum(
            jnp.dot(
                hot[e],
                table_ref[pl.ds((e * blocks + z) * PADDED, PADDED), :],
                preferred_element_type=jnp.float32,
            )
            for e in range(2)
        )
        mixed = (tokens_ref[:, cols].astype(jnp.float32) + gate * picked).astype(jnp.bfloat16)
        mixed_ref[:, cols] = mixed
        values = mixed.astype(jnp.float32)
        for i in range(block_width // LANES):
            part = values[:, i * LANES : (i + 1) * LANES]
            square += part * part
    mean = jnp.sum(square, axis=1, keepdims=True) * (1.0 / width)
    scale = lax.rsqrt(mean + 1e-05)
    for z in range(blocks):
        cols = pl.ds(z * block_width, block_width)
        values = mixed_ref[:, cols].astype(jnp.float32)
        normed_ref[:, cols] = (values * scale * gain_ref[:, cols]).astype(jnp.bfloat16)
    for load in loads:
        load.wait()
    cores, ys, rows = w_ref.shape[1:4]
    pair = 2 * cores * rows
    query = jnp.zeros(query_ref.shape, jnp.float32)
    for x in range(0, parts, 2):
        for y in range(ys):
            block = jnp.concatenate([w_ref[x + i, c, y] for i in range(2) for c in range(cores)], axis=0)
            start = (y * parts + x) * cores * rows
            query += jnp.dot(
                normed_ref[:, start : start + pair], block, preferred_element_type=jnp.float32
            )
    query_ref[...] = query.astype(query_ref.dtype)


def finish(tokens, table, column, gate, gain, w_query):
    vmem = pl.BlockSpec(memory_space=pltpu.VMEM)
    tok_count, width = tokens.shape
    columns = w_query.shape[-1]
    return pl.pallas_call(
        finish_kernel,
        out_shape=(
            jax.ShapeDtypeStruct((tok_count, width), jnp.bfloat16),
            jax.ShapeDtypeStruct((tok_count, columns), jnp.bfloat16),
        ),
        in_specs=[vmem] * 5 + [pl.BlockSpec(memory_space=pl.ANY)],
        out_specs=(vmem, vmem),
        scratch_shapes=[
            pltpu.VMEM((tok_count, width), jnp.bfloat16),
            pltpu.VMEM(w_query.shape, jnp.bfloat16),
            pltpu.SemaphoreType.DMA((w_query.shape[0],)),
        ],
        compiler_params=pltpu.CompilerParams(vmem_limit_bytes=24 * 1024 * 1024),
        cost_estimate=pl.CostEstimate(
            flops=2 * tok_count * width * columns, bytes_accessed=4 * width * columns, transcendentals=0
        ),
    )(tokens, table, column[:, None], gate[:, None], gain[None, :], w_query)


def local(
    tokens,
    first_expert,
    first_slot,
    second_expert,
    second_slot,
    first_gate,
    second_gate,
    w_gate,
    w_up,
    w_down,
    norm_gain,
    w_query,
):
    tok_count, width = tokens.shape
    blocks = lax.axis_size("z")
    chips = lax.axis_size(CHIPS)
    block_width = width // blocks
    units = w_gate.shape[1]
    own_expert = lax.axis_index("y_lo")
    own_block = lax.axis_index("z")

    served_first = first_slot >= 0
    served = served_first | (second_slot >= 0)
    expert_of = jnp.where(served_first, first_expert, second_expert)
    slot_of = jnp.where(served_first, first_slot, second_slot + CAP1)
    gate_of = jnp.where(served_first, first_gate, second_gate)

    token_block = lax.dynamic_slice_in_dim(tokens, own_block * block_width, block_width, 1)
    placement = jnp.where(served & (expert_of == own_expert), slot_of, -1)
    slot_hot = (jnp.arange(SLOTS, dtype=jnp.int32)[:, None] == placement[None, :]).astype(jnp.bfloat16)
    slot_rows = jnp.dot(slot_hot, token_block, preferred_element_type=jnp.float32).astype(jnp.bfloat16)

    slot_copies, w_query = tie(copies(slot_rows, CHIPS), w_query)
    rows = exchange(slot_copies, CHIPS).reshape(chips * SLOTS, block_width)
    w_gate_other = other_core(w_gate)
    w_up_other = other_core(w_up)
    query_rows = [w_query, along("y_hi", w_query, -1)]

    partial = jnp.concatenate(
        [
            jnp.dot(rows, w, preferred_element_type=jnp.float32).astype(jnp.bfloat16)
            for w in (w_gate, w_gate_other, w_up, w_up_other)
        ],
        axis=1,
    )
    share = chips * SLOTS // blocks
    partial, *query_rows = tie(partial, *query_rows)
    summed = exchange(partial.reshape(blocks, share, 4 * units), "z")
    query_rows += [along("y_hi", query_rows[0], -2), along("y_hi", query_rows[0], -3)]
    summed = jnp.sum(summed.astype(jnp.float32), axis=0)
    hidden_share = (jax.nn.silu(summed[:, : 2 * units]) * summed[:, 2 * units :]).astype(jnp.bfloat16)
    hidden_copies, *query_rows = tie(copies(hidden_share, "z"), *query_rows)
    for bit in (1, 2):
        turned = query_rows[-bit:] + query_rows[:-bit]
        set_bit = (lax.axis_index("y_hi") & bit) != 0
        query_rows = [jnp.where(set_bit, t, q) for t, q in zip(turned, query_rows, strict=True)]
    column_rows = jnp.stack(query_rows)
    w_query_full = lax.all_gather(column_rows, ("x", "core"), axis=0)
    w_query_full = w_query_full.reshape((-1, 2) + column_rows.shape)
    hidden = exchange(hidden_copies, "z").reshape(chips * SLOTS, 2 * units)
    w_down_other = other_core(w_down)
    out_part = jnp.dot(hidden[:, :units], w_down, preferred_element_type=jnp.float32) + jnp.dot(
        hidden[:, units:], w_down_other, preferred_element_type=jnp.float32
    )
    out_part = out_part.astype(jnp.bfloat16)
    pieces = exchange(out_part.reshape(chips, SLOTS, block_width), CHIPS)
    expert_out = jnp.sum(pieces.astype(jnp.float32), axis=0).astype(jnp.bfloat16)
    expert_out = jnp.concatenate([expert_out, jnp.zeros((PADDED - SLOTS, block_width), jnp.bfloat16)], 0)
    table = exchange(copies(expert_out, EXPERT), EXPERT).reshape(-1, block_width)

    column = jnp.where(served, expert_of * PADDED + slot_of, -1)
    return finish(tokens, table, column, gate_of, norm_gain, w_query_full)


def solution(mesh):
    fine = Mesh(mesh.devices.reshape(tuple(SIZES.values())), tuple(SIZES))
    in_specs = (
        P(DP, None),
        P(DP),
        P(DP),
        P(DP),
        P(DP),
        P(DP),
        P(DP),
        P(EXPERT, DP),
        P(EXPERT, DP),
        P(DP, EXPERT),
        P(),
        P(DP, EXPERT),
    )
    out_specs = (P(DP, None), P(DP, EXPERT))
    return jax.shard_map(local, mesh=fine, in_specs=in_specs, out_specs=out_specs, check_vma=False)
```

```python
import jax
import jax.numpy as jnp
from jax import lax
from jax.experimental import pallas as pl
from jax.experimental.pallas import tpu as pltpu
from jax.sharding import Mesh, PartitionSpec as P

CAP1 = 4
CAP2 = 2
SLOTS = CAP1 + CAP2
EXPERT = ("y_lo", "z")
CHIPS = ("y_hi", "x")
DP = ("y_hi", "x", "core")
SIZES = {"y_lo": 2, "z": 8, "y_hi": 4, "x": 8, "core": 2}
PADDED = 8
LANES = 128


def exchange(blocks, axes):
    return lax.all_to_all(blocks, axes, split_axis=0, concat_axis=0, tiled=True)


def other_core(block):
    return lax.ppermute(block, "core", [(0, 1), (1, 0)])


def across(block, bit):
    return lax.ppermute(block, "y_hi", [(i, i ^ bit) for i in range(lax.axis_size("y_hi"))])


def in_order(own, other, bit):
    upper = (lax.axis_index("y_hi") & bit) != 0
    return jnp.concatenate([jnp.where(upper, other, own), jnp.where(upper, own, other)], axis=0)


def tie(*values):
    return lax.optimization_barrier(values)


def small_call(kernel, shape, vmem_count, *operands, scratch=()):
    vmem = pl.BlockSpec(memory_space=pltpu.VMEM)
    outside = len(operands) - vmem_count
    size = 1
    for extent in shape:
        size *= extent
    return pl.pallas_call(
        kernel,
        out_shape=jax.ShapeDtypeStruct(shape, jnp.bfloat16),
        in_specs=[pl.BlockSpec(memory_space=pltpu.HBM)] * outside + [vmem] * vmem_count,
        out_specs=vmem,
        scratch_shapes=list(scratch),
        compiler_params=pltpu.CompilerParams(vmem_limit_bytes=16 * 1024 * 1024),
        cost_estimate=pl.CostEstimate(flops=2 * size, bytes_accessed=4 * size, transcendentals=0),
    )(*operands)


def slots_kernel(tokens_hbm, expert_ref, slot_ref, out_ref, block_ref, sem):
    width = block_ref.shape[1]
    start = pl.multiple_of(lax.axis_index("z") * width, LANES)
    load = pltpu.make_async_copy(tokens_hbm.at[:, pl.ds(start, width)], block_ref, sem)
    load.start()
    placement = jnp.where(expert_ref[...] == lax.axis_index("y_lo"), slot_ref[...], -1)
    slots = lax.broadcasted_iota(jnp.int32, (PADDED, placement.shape[1]), 0)
    hot = (slots == placement).astype(jnp.bfloat16)
    load.wait()
    rows = jnp.dot(hot, block_ref[...], preferred_element_type=jnp.float32).astype(jnp.bfloat16)
    for i in range(out_ref.shape[0]):
        out_ref[i] = rows[:SLOTS]


def products_kernel(rows_ref, *refs):
    out_ref = refs[-1]
    rows = rows_ref[...]
    units = refs[0].shape[1]
    for i, w_ref in enumerate(refs[:-1]):
        out_ref[:, i * units : (i + 1) * units] = jnp.dot(
            rows, w_ref[...], preferred_element_type=jnp.float32
        ).astype(jnp.bfloat16)


def hidden_kernel(parts_ref, out_ref):
    units = out_ref.shape[2]
    total = parts_ref[0].astype(jnp.float32)
    for i in range(1, parts_ref.shape[0]):
        total += parts_ref[i].astype(jnp.float32)
    gate, up = total[:, :units], total[:, units:]
    hidden = (gate / (1.0 + jnp.exp(-gate)) * up).astype(jnp.bfloat16)
    for i in range(out_ref.shape[0]):
        out_ref[i] = hidden


def total_kernel(parts_ref, out_ref):
    total = parts_ref[0].astype(jnp.float32)
    for i in range(1, parts_ref.shape[0]):
        total += parts_ref[i].astype(jnp.float32)
    rows = jnp.concatenate([total, jnp.zeros((PADDED - SLOTS, total.shape[1]), jnp.float32)], axis=0)
    rows = rows.astype(jnp.bfloat16)
    for i in range(out_ref.shape[0]):
        out_ref[i] = rows


def finish_kernel(
    tokens_ref, table_ref, column_ref, gate_ref, gain_ref, w_hbm, mixed_ref, query_ref, normed_ref, w_ref, sem
):
    parts = w_ref.shape[0]
    loads = [pltpu.make_async_copy(w_hbm.at[i], w_ref.at[i], sem.at[i]) for i in range(parts)]
    for load in loads:
        load.start()
    blocks = table_ref.shape[0] // (2 * PADDED)
    tok_count, width = tokens_ref.shape
    block_width = width // blocks
    column = column_ref[...]
    slots = lax.broadcasted_iota(jnp.int32, (tok_count, PADDED), 1)
    hot = [(column == slots + e * PADDED).astype(jnp.bfloat16) for e in range(2)]
    gate = gate_ref[...]
    square = jnp.zeros((tok_count, LANES), jnp.float32)
    for z in range(blocks):
        cols = pl.ds(z * block_width, block_width)
        picked = sum(
            jnp.dot(
                hot[e],
                table_ref[pl.ds((e * blocks + z) * PADDED, PADDED), :],
                preferred_element_type=jnp.float32,
            )
            for e in range(2)
        )
        mixed = (tokens_ref[:, cols].astype(jnp.float32) + gate * picked).astype(jnp.bfloat16)
        mixed_ref[:, cols] = mixed
        values = mixed.astype(jnp.float32)
        for i in range(block_width // LANES):
            part = values[:, i * LANES : (i + 1) * LANES]
            square += part * part
    mean = jnp.sum(square, axis=1, keepdims=True) * (1.0 / width)
    scale = lax.rsqrt(mean + 1e-05)
    for z in range(blocks):
        cols = pl.ds(z * block_width, block_width)
        values = mixed_ref[:, cols].astype(jnp.float32)
        normed_ref[:, cols] = (values * scale * gain_ref[:, cols]).astype(jnp.bfloat16)
    for load in loads:
        load.wait()
    cores, ys, rows = w_ref.shape[1:4]
    pair = 2 * cores * rows
    query = jnp.zeros(query_ref.shape, jnp.float32)
    for x in range(0, parts, 2):
        for y in range(ys):
            block = jnp.concatenate([w_ref[x + i, c, y] for i in range(2) for c in range(cores)], axis=0)
            start = (y * parts + x) * cores * rows
            query += jnp.dot(
                normed_ref[:, start : start + pair], block, preferred_element_type=jnp.float32
            )
    query_ref[...] = query.astype(query_ref.dtype)


def finish(tokens, table, column, gate, gain, w_query):
    vmem = pl.BlockSpec(memory_space=pltpu.VMEM)
    tok_count, width = tokens.shape
    columns = w_query.shape[-1]
    return pl.pallas_call(
        finish_kernel,
        out_shape=(
            jax.ShapeDtypeStruct((tok_count, width), jnp.bfloat16),
            jax.ShapeDtypeStruct((tok_count, columns), jnp.bfloat16),
        ),
        in_specs=[vmem] * 5 + [pl.BlockSpec(memory_space=pltpu.HBM)],
        out_specs=(vmem, vmem),
        scratch_shapes=[
            pltpu.VMEM((tok_count, width), jnp.bfloat16),
            pltpu.VMEM(w_query.shape, jnp.bfloat16),
            pltpu.SemaphoreType.DMA((w_query.shape[0],)),
        ],
        compiler_params=pltpu.CompilerParams(vmem_limit_bytes=24 * 1024 * 1024),
        cost_estimate=pl.CostEstimate(
            flops=2 * tok_count * width * columns, bytes_accessed=4 * width * columns, transcendentals=0
        ),
    )(tokens, table, column[:, None], gate[:, None], gain[None, :], w_query)


def local(
    tokens,
    first_expert,
    first_slot,
    second_expert,
    second_slot,
    first_gate,
    second_gate,
    w_gate,
    w_up,
    w_down,
    norm_gain,
    w_query,
):
    tok_count, width = tokens.shape
    blocks = lax.axis_size("z")
    chips = lax.axis_size(CHIPS)
    block_width = width // blocks
    units = w_gate.shape[1]
    experts = lax.axis_size("y_lo")

    served_first = first_slot >= 0
    served = served_first | (second_slot >= 0)
    expert_of = jnp.where(served_first, first_expert, second_expert)
    slot_of = jnp.where(served_first, first_slot, second_slot + CAP1)
    gate_of = jnp.where(served_first, first_gate, second_gate)

    slot_copies = small_call(
        slots_kernel,
        (chips, SLOTS, block_width),
        2,
        tokens,
        expert_of[None, :],
        jnp.where(served, slot_of, -1)[None, :],
        scratch=(pltpu.VMEM((tok_count, block_width), jnp.bfloat16), pltpu.SemaphoreType.DMA(())),
    )
    slot_copies, w_query = tie(slot_copies, w_query)
    rows = exchange(slot_copies, CHIPS).reshape(chips * SLOTS, block_width)
    w_gate_other = other_core(w_gate)
    w_up_other = other_core(w_up)
    w_query_beside = across(w_query, 1)

    partial = small_call(
        products_kernel, (chips * SLOTS, 4 * units), 5, rows, w_gate, w_gate_other, w_up, w_up_other
    )
    share = chips * SLOTS // blocks
    partial, w_query, w_query_beside = tie(partial, w_query, w_query_beside)
    summed = exchange(partial.reshape(blocks, share, 4 * units), "z")
    query_rows = in_order(w_query, w_query_beside, 1)
    query_rows_other = across(query_rows, 2)
    hidden_copies = small_call(hidden_kernel, (blocks, share, 2 * units), 1, summed)
    hidden_copies, query_rows_other = tie(hidden_copies, query_rows_other)
    column_rows = in_order(query_rows, query_rows_other, 2).reshape((-1,) + w_query.shape)
    w_query_full = lax.all_gather(column_rows, ("x", "core"), axis=0)
    w_query_full = w_query_full.reshape((-1, 2) + column_rows.shape)
    hidden = exchange(hidden_copies, "z").reshape(chips * SLOTS, 2 * units)
    w_down_other = other_core(w_down)
    out_part = jnp.dot(hidden[:, :units], w_down, preferred_element_type=jnp.float32) + jnp.dot(
        hidden[:, units:], w_down_other, preferred_element_type=jnp.float32
    )
    out_part = out_part.astype(jnp.bfloat16)
    pieces = exchange(out_part.reshape(chips, SLOTS, block_width), CHIPS)
    out_copies = small_call(total_kernel, (experts * blocks, PADDED, block_width), 1, pieces)
    table = exchange(out_copies, EXPERT).reshape(-1, block_width)

    column = jnp.where(served, expert_of * PADDED + slot_of, -1)
    return finish(tokens, table, column, gate_of, norm_gain, w_query_full)


def solution(mesh):
    fine = Mesh(mesh.devices.reshape(tuple(SIZES.values())), tuple(SIZES))
    in_specs = (
        P(DP, None),
        P(DP),
        P(DP),
        P(DP),
        P(DP),
        P(DP),
        P(DP),
        P(EXPERT, DP),
        P(EXPERT, DP),
        P(DP, EXPERT),
        P(),
        P(DP, EXPERT),
    )
    out_specs = (P(DP, None), P(DP, EXPERT))
    return jax.shard_map(local, mesh=fine, in_specs=in_specs, out_specs=out_specs, check_vma=False)
```

```python
import jax
import jax.numpy as jnp
from jax import lax
from jax.experimental import pallas as pl
from jax.experimental.pallas import tpu as pltpu
from jax.sharding import Mesh, PartitionSpec as P

CAP1 = 4
CAP2 = 2
SLOTS = CAP1 + CAP2
EXPERT = ("y_lo", "z")
CHIPS = ("y_hi", "x")
DP = ("y_hi", "x", "core")
SIZES = {"y_lo": 2, "z": 8, "y_hi": 4, "x": 8, "core": 2}
PADDED = 8
LANES = 128
VMEM_BYTES = 60 * 1024 * 1024
FINISH_BYTES = 50 * 1024 * 1024


def exchange(blocks, axes):
    return lax.all_to_all(blocks, axes, split_axis=0, concat_axis=0, tiled=True)


def other_core(block):
    return lax.ppermute(block, "core", [(0, 1), (1, 0)])


def across(block, bit):
    return lax.ppermute(block, "y_hi", [(i, i ^ bit) for i in range(lax.axis_size("y_hi"))])


def in_order(own, other, bit):
    upper = (lax.axis_index("y_hi") & bit) != 0
    return jnp.concatenate([jnp.where(upper, other, own), jnp.where(upper, own, other)], axis=0)


def tie(*values):
    return lax.optimization_barrier(values)


def small_call(kernel, shape, vmem_count, *operands, scratch=()):
    vmem = pl.BlockSpec(memory_space=pltpu.VMEM)
    outside = len(operands) - vmem_count
    size = 1
    for extent in shape:
        size *= extent
    return pl.pallas_call(
        kernel,
        out_shape=jax.ShapeDtypeStruct(shape, jnp.bfloat16),
        in_specs=[pl.BlockSpec(memory_space=pltpu.HBM)] * outside + [vmem] * vmem_count,
        out_specs=vmem,
        scratch_shapes=list(scratch),
        compiler_params=pltpu.CompilerParams(vmem_limit_bytes=VMEM_BYTES if outside else VMEM_BYTES // 4),
        cost_estimate=pl.CostEstimate(flops=2 * size, bytes_accessed=4 * size, transcendentals=0),
    )(*operands)


def slots_kernel(
    tokens_hbm, first_expert_ref, first_slot_ref, second_expert_ref, second_slot_ref, out_ref, block_ref, sem
):
    width = block_ref.shape[1]
    start = pl.multiple_of(lax.axis_index("z") * width, LANES)
    load = pltpu.make_async_copy(tokens_hbm.at[:, pl.ds(start, width)], block_ref, sem)
    load.start()
    own = lax.axis_index("y_lo")
    first, second = first_slot_ref[...], second_slot_ref[...]
    placement = jnp.where((second_expert_ref[...] == own) & (second >= 0), second + CAP1, -1)
    placement = jnp.where((first_expert_ref[...] == own) & (first >= 0), first, placement)
    slots = lax.broadcasted_iota(jnp.int32, (PADDED, placement.shape[1]), 0)
    hot = (slots == placement).astype(jnp.bfloat16)
    load.wait()
    rows = jnp.dot(hot, block_ref[...], preferred_element_type=jnp.float32).astype(jnp.bfloat16)
    for i in range(out_ref.shape[0]):
        out_ref[i] = rows[:SLOTS]


def products_kernel(rows_ref, *refs):
    out_ref = refs[-1]
    rows = rows_ref[...]
    units = refs[0].shape[1]
    for i, w_ref in enumerate(refs[:-1]):
        out_ref[:, i * units : (i + 1) * units] = jnp.dot(
            rows, w_ref[...], preferred_element_type=jnp.float32
        ).astype(jnp.bfloat16)


def hidden_kernel(parts_ref, out_ref):
    units = out_ref.shape[2]
    total = parts_ref[0].astype(jnp.float32)
    for i in range(1, parts_ref.shape[0]):
        total += parts_ref[i].astype(jnp.float32)
    gate, up = total[:, :units], total[:, units:]
    hidden = (gate / (1.0 + jnp.exp(-gate)) * up).astype(jnp.bfloat16)
    for i in range(out_ref.shape[0]):
        out_ref[i] = hidden


def total_kernel(parts_ref, out_ref):
    total = parts_ref[0].astype(jnp.float32)
    for i in range(1, parts_ref.shape[0]):
        total += parts_ref[i].astype(jnp.float32)
    rows = jnp.concatenate([total, jnp.zeros((PADDED - SLOTS, total.shape[1]), jnp.float32)], axis=0)
    rows = rows.astype(jnp.bfloat16)
    for i in range(out_ref.shape[0]):
        out_ref[i] = rows


def finish_kernel(
    tokens_ref, table_ref, column_ref, gate_ref, gain_ref, w_hbm, mixed_ref, query_ref, normed_ref, w_ref, sem
):
    parts = w_ref.shape[0]
    loads = [pltpu.make_async_copy(w_hbm.at[i], w_ref.at[i], sem.at[i]) for i in range(parts)]
    for load in loads:
        load.start()
    blocks = table_ref.shape[0] // (2 * PADDED)
    tok_count, width = tokens_ref.shape
    block_width = width // blocks
    column = column_ref[...]
    slots = lax.broadcasted_iota(jnp.int32, (tok_count, PADDED), 1)
    hot = [(column == slots + e * PADDED).astype(jnp.bfloat16) for e in range(2)]
    gate = gate_ref[...]
    square = jnp.zeros((tok_count, LANES), jnp.float32)
    for z in range(blocks):
        cols = pl.ds(z * block_width, block_width)
        picked = sum(
            jnp.dot(
                hot[e],
                table_ref[pl.ds((e * blocks + z) * PADDED, PADDED), :],
                preferred_element_type=jnp.float32,
            )
            for e in range(2)
        )
        mixed = (tokens_ref[:, cols].astype(jnp.float32) + gate * picked).astype(jnp.bfloat16)
        mixed_ref[:, cols] = mixed
        values = mixed.astype(jnp.float32)
        for i in range(block_width // LANES):
            part = values[:, i * LANES : (i + 1) * LANES]
            square += part * part
    mean = jnp.sum(square, axis=1, keepdims=True) * (1.0 / width)
    scale = lax.rsqrt(mean + 1e-05)
    for z in range(blocks):
        cols = pl.ds(z * block_width, block_width)
        values = mixed_ref[:, cols].astype(jnp.float32)
        normed_ref[:, cols] = (values * scale * gain_ref[:, cols]).astype(jnp.bfloat16)
    for load in loads:
        load.wait()
    cores, ys, rows = w_ref.shape[1:4]
    pair = 2 * cores * rows
    query = jnp.zeros(query_ref.shape, jnp.float32)
    for x in range(0, parts, 2):
        for y in range(ys):
            block = jnp.concatenate([w_ref[x + i, c, y] for i in range(2) for c in range(cores)], axis=0)
            start = (y * parts + x) * cores * rows
            query += jnp.dot(
                normed_ref[:, start : start + pair], block, preferred_element_type=jnp.float32
            )
    query_ref[...] = query.astype(query_ref.dtype)


def finish(tokens, table, column, gate, gain, w_query):
    vmem = pl.BlockSpec(memory_space=pltpu.VMEM)
    tok_count, width = tokens.shape
    columns = w_query.shape[-1]
    return pl.pallas_call(
        finish_kernel,
        out_shape=(
            jax.ShapeDtypeStruct((tok_count, width), jnp.bfloat16),
            jax.ShapeDtypeStruct((tok_count, columns), jnp.bfloat16),
        ),
        in_specs=[vmem] * 5 + [pl.BlockSpec(memory_space=pltpu.HBM)],
        out_specs=(vmem, vmem),
        scratch_shapes=[
            pltpu.VMEM((tok_count, width), jnp.bfloat16),
            pltpu.VMEM(w_query.shape, jnp.bfloat16),
            pltpu.SemaphoreType.DMA((w_query.shape[0],)),
        ],
        compiler_params=pltpu.CompilerParams(vmem_limit_bytes=FINISH_BYTES),
        cost_estimate=pl.CostEstimate(
            flops=2 * tok_count * width * columns, bytes_accessed=4 * width * columns, transcendentals=0
        ),
    )(tokens, table, column[:, None], gate[:, None], gain[None, :], w_query)


def local(
    tokens,
    first_expert,
    first_slot,
    second_expert,
    second_slot,
    first_gate,
    second_gate,
    w_gate,
    w_up,
    w_down,
    norm_gain,
    w_query,
):
    tok_count, width = tokens.shape
    blocks = lax.axis_size("z")
    chips = lax.axis_size(CHIPS)
    block_width = width // blocks
    units = w_gate.shape[1]
    experts = lax.axis_size("y_lo")

    served_first = first_slot >= 0
    served = served_first | (second_slot >= 0)
    expert_of = jnp.where(served_first, first_expert, second_expert)
    slot_of = jnp.where(served_first, first_slot, second_slot + CAP1)
    gate_of = jnp.where(served_first, first_gate, second_gate)

    slot_copies = small_call(
        slots_kernel,
        (chips, SLOTS, block_width),
        4,
        tokens,
        first_expert[None, :],
        first_slot[None, :],
        second_expert[None, :],
        second_slot[None, :],
        scratch=(pltpu.VMEM((tok_count, block_width), jnp.bfloat16), pltpu.SemaphoreType.DMA(())),
    )
    slot_copies, w_query = tie(slot_copies, w_query)
    rows = exchange(slot_copies, CHIPS).reshape(chips * SLOTS, block_width)
    w_gate_other = other_core(w_gate)
    w_up_other = other_core(w_up)
    w_query_beside = across(w_query, 1)

    partial = small_call(
        products_kernel, (chips * SLOTS, 4 * units), 5, rows, w_gate, w_gate_other, w_up, w_up_other
    )
    share = chips * SLOTS // blocks
    partial, w_query, w_query_beside = tie(partial, w_query, w_query_beside)
    summed = exchange(partial.reshape(blocks, share, 4 * units), "z")
    query_rows = in_order(w_query, w_query_beside, 1)
    query_rows_other = across(query_rows, 2)
    hidden_copies = small_call(hidden_kernel, (blocks, share, 2 * units), 1, summed)
    hidden_copies, query_rows_other = tie(hidden_copies, query_rows_other)
    query_rows = in_order(query_rows, query_rows_other, 2).reshape((-1,) + w_query.shape)
    w_query_full = lax.all_gather(query_rows, ("x", "core"), axis=0)
    w_query_full = w_query_full.reshape((-1, 2) + query_rows.shape)
    hidden = exchange(hidden_copies, "z").reshape(chips * SLOTS, 2 * units)
    w_down_other = other_core(w_down)
    out_part = jnp.dot(hidden[:, :units], w_down, preferred_element_type=jnp.float32) + jnp.dot(
        hidden[:, units:], w_down_other, preferred_element_type=jnp.float32
    )
    out_part = out_part.astype(jnp.bfloat16)
    pieces = exchange(out_part.reshape(chips, SLOTS, block_width), CHIPS)
    out_copies = small_call(total_kernel, (experts * blocks, PADDED, block_width), 1, pieces)
    table = exchange(out_copies, EXPERT).reshape(-1, block_width)

    column = jnp.where(served, expert_of * PADDED + slot_of, -1)
    return finish(tokens, table, column, gate_of, norm_gain, w_query_full)


def solution(mesh):
    fine = Mesh(mesh.devices.reshape(tuple(SIZES.values())), tuple(SIZES))
    in_specs = (
        P(DP, None),
        P(DP),
        P(DP),
        P(DP),
        P(DP),
        P(DP),
        P(DP),
        P(EXPERT, DP),
        P(EXPERT, DP),
        P(DP, EXPERT),
        P(),
        P(DP, EXPERT),
    )
    out_specs = (P(DP, None), P(DP, EXPERT))
    return jax.shard_map(local, mesh=fine, in_specs=in_specs, out_specs=out_specs, check_vma=False)
```

```python
import jax
import jax.numpy as jnp
from jax import lax
from jax.experimental import pallas as pl
from jax.experimental.pallas import tpu as pltpu
from jax.sharding import Mesh, PartitionSpec as P

CAP1 = 4
CAP2 = 2
SLOTS = CAP1 + CAP2
EXPERT = ("y_lo", "z")
CHIPS = ("y_hi", "x")
DP = ("y_hi", "x", "core")
SIZES = {"y_lo": 2, "z": 8, "y_hi": 4, "x": 8, "core": 2}
PADDED = 8
LANES = 128
VMEM_BYTES = 60 * 1024 * 1024
FINISH_BYTES = 50 * 1024 * 1024


def exchange(blocks, axes):
    return lax.all_to_all(blocks, axes, split_axis=0, concat_axis=0, tiled=True)


def other_core(block):
    return lax.ppermute(block, "core", [(0, 1), (1, 0)])


def across(block, bit):
    return lax.ppermute(block, "y_hi", [(i, i ^ bit) for i in range(lax.axis_size("y_hi"))])


def in_order(own, other, bit):
    upper = (lax.axis_index("y_hi") & bit) != 0
    return jnp.concatenate([jnp.where(upper, other, own), jnp.where(upper, own, other)], axis=0)


def tie(*values):
    return lax.optimization_barrier(values)


def small_call(kernel, shape, vmem_count, *operands, scratch=()):
    vmem = pl.BlockSpec(memory_space=pltpu.VMEM)
    outside = len(operands) - vmem_count
    size = 1
    for extent in shape:
        size *= extent
    return pl.pallas_call(
        kernel,
        out_shape=jax.ShapeDtypeStruct(shape, jnp.bfloat16),
        in_specs=[pl.BlockSpec(memory_space=pltpu.HBM)] * outside + [vmem] * vmem_count,
        out_specs=vmem,
        scratch_shapes=list(scratch),
        compiler_params=pltpu.CompilerParams(vmem_limit_bytes=VMEM_BYTES if outside else VMEM_BYTES // 4),
        cost_estimate=pl.CostEstimate(flops=2 * size, bytes_accessed=4 * size, transcendentals=0),
    )(*operands)


def slots_kernel(
    tokens_hbm, first_expert_ref, first_slot_ref, second_expert_ref, second_slot_ref, out_ref, block_ref, sem
):
    width = block_ref.shape[1]
    start = pl.multiple_of(lax.axis_index("z") * width, LANES)
    load = pltpu.make_async_copy(tokens_hbm.at[:, pl.ds(start, width)], block_ref, sem)
    load.start()
    own = lax.axis_index("y_lo")
    first, second = first_slot_ref[...], second_slot_ref[...]
    placement = jnp.where((second_expert_ref[...] == own) & (second >= 0), second + CAP1, -1)
    placement = jnp.where((first_expert_ref[...] == own) & (first >= 0), first, placement)
    slots = lax.broadcasted_iota(jnp.int32, (PADDED, placement.shape[1]), 0)
    hot = (slots == placement).astype(jnp.bfloat16)
    load.wait()
    rows = jnp.dot(hot, block_ref[...], preferred_element_type=jnp.float32).astype(jnp.bfloat16)
    for i in range(out_ref.shape[0]):
        out_ref[i] = rows[:SLOTS]


def products_kernel(rows_ref, own_ref, gate_other_ref, up_other_ref, out_ref):
    rows = rows_ref[...]
    units = gate_other_ref.shape[1]

    def product(at, w):
        out_ref[:, at * units : (at + 1) * units] = jnp.dot(
            rows, w, preferred_element_type=jnp.float32
        ).astype(jnp.bfloat16)

    product(0, own_ref[:, :units])
    product(1, gate_other_ref[...])
    product(2, own_ref[:, units:])
    product(3, up_other_ref[...])


def hidden_kernel(parts_ref, out_ref):
    units = out_ref.shape[2]
    total = parts_ref[0].astype(jnp.float32)
    for i in range(1, parts_ref.shape[0]):
        total += parts_ref[i].astype(jnp.float32)
    gate, up = total[:, :units], total[:, units:]
    hidden = (gate / (1.0 + jnp.exp(-gate)) * up).astype(jnp.bfloat16)
    for i in range(out_ref.shape[0]):
        out_ref[i] = hidden


def total_kernel(parts_ref, out_ref):
    total = parts_ref[0].astype(jnp.float32)
    for i in range(1, parts_ref.shape[0]):
        total += parts_ref[i].astype(jnp.float32)
    rows = jnp.concatenate([total, jnp.zeros((PADDED - SLOTS, total.shape[1]), jnp.float32)], axis=0)
    rows = rows.astype(jnp.bfloat16)
    for i in range(out_ref.shape[0]):
        out_ref[i] = rows


def finish_kernel(
    tokens_ref, table_ref, column_ref, gate_ref, gain_ref, w_hbm, mixed_ref, query_ref, normed_ref, w_ref, sem
):
    parts = w_ref.shape[0]
    loads = [pltpu.make_async_copy(w_hbm.at[i], w_ref.at[i], sem.at[i]) for i in range(parts)]
    for load in loads:
        load.start()
    blocks = table_ref.shape[0] // (2 * PADDED)
    tok_count, width = tokens_ref.shape
    block_width = width // blocks
    column = column_ref[...]
    slots = lax.broadcasted_iota(jnp.int32, (tok_count, PADDED), 1)
    hot = [(column == slots + e * PADDED).astype(jnp.bfloat16) for e in range(2)]
    gate = gate_ref[...]
    square = jnp.zeros((tok_count, LANES), jnp.float32)
    for z in range(blocks):
        cols = pl.ds(z * block_width, block_width)
        picked = sum(
            jnp.dot(
                hot[e],
                table_ref[pl.ds((e * blocks + z) * PADDED, PADDED), :],
                preferred_element_type=jnp.float32,
            )
            for e in range(2)
        )
        mixed = (tokens_ref[:, cols].astype(jnp.float32) + gate * picked).astype(jnp.bfloat16)
        mixed_ref[:, cols] = mixed
        values = mixed.astype(jnp.float32)
        for i in range(block_width // LANES):
            part = values[:, i * LANES : (i + 1) * LANES]
            square += part * part
    mean = jnp.sum(square, axis=1, keepdims=True) * (1.0 / width)
    scale = lax.rsqrt(mean + 1e-05)
    for z in range(blocks):
        cols = pl.ds(z * block_width, block_width)
        values = mixed_ref[:, cols].astype(jnp.float32)
        normed_ref[:, cols] = (values * scale * gain_ref[:, cols]).astype(jnp.bfloat16)
    for load in loads:
        load.wait()
    cores, ys, rows = w_ref.shape[1:4]
    pair = 2 * cores * rows
    query = jnp.zeros(query_ref.shape, jnp.float32)
    for x in range(0, parts, 2):
        for y in range(ys):
            block = jnp.concatenate([w_ref[x + i, c, y] for i in range(2) for c in range(cores)], axis=0)
            start = (y * parts + x) * cores * rows
            query += jnp.dot(
                normed_ref[:, start : start + pair], block, preferred_element_type=jnp.float32
            )
    query_ref[...] = query.astype(query_ref.dtype)


def finish(tokens, table, column, gate, gain, w_query):
    vmem = pl.BlockSpec(memory_space=pltpu.VMEM)
    tok_count, width = tokens.shape
    columns = w_query.shape[-1]
    return pl.pallas_call(
        finish_kernel,
        out_shape=(
            jax.ShapeDtypeStruct((tok_count, width), jnp.bfloat16),
            jax.ShapeDtypeStruct((tok_count, columns), jnp.bfloat16),
        ),
        in_specs=[vmem] * 5 + [pl.BlockSpec(memory_space=pltpu.HBM)],
        out_specs=(vmem, vmem),
        scratch_shapes=[
            pltpu.VMEM((tok_count, width), jnp.bfloat16),
            pltpu.VMEM(w_query.shape, jnp.bfloat16),
            pltpu.SemaphoreType.DMA((w_query.shape[0],)),
        ],
        compiler_params=pltpu.CompilerParams(vmem_limit_bytes=FINISH_BYTES),
        cost_estimate=pl.CostEstimate(
            flops=2 * tok_count * width * columns, bytes_accessed=4 * width * columns, transcendentals=0
        ),
    )(tokens, table, column[:, None], gate[:, None], gain[None, :], w_query)


def local(
    tokens,
    first_expert,
    first_slot,
    second_expert,
    second_slot,
    first_gate,
    second_gate,
    w_gate,
    w_up,
    w_down,
    norm_gain,
    w_query,
):
    tok_count, width = tokens.shape
    blocks = lax.axis_size("z")
    chips = lax.axis_size(CHIPS)
    block_width = width // blocks
    units = w_gate.shape[1]
    experts = lax.axis_size("y_lo")

    served_first = first_slot >= 0
    served = served_first | (second_slot >= 0)
    expert_of = jnp.where(served_first, first_expert, second_expert)
    slot_of = jnp.where(served_first, first_slot, second_slot + CAP1)
    gate_of = jnp.where(served_first, first_gate, second_gate)

    slot_copies = small_call(
        slots_kernel,
        (chips, SLOTS, block_width),
        4,
        tokens,
        first_expert[None, :],
        first_slot[None, :],
        second_expert[None, :],
        second_slot[None, :],
        scratch=(pltpu.VMEM((tok_count, block_width), jnp.bfloat16), pltpu.SemaphoreType.DMA(())),
    )
    query_rows = in_order(w_query, across(w_query, 1), 1)
    slot_copies, query_rows = tie(slot_copies, query_rows)
    rows = exchange(slot_copies, CHIPS).reshape(chips * SLOTS, block_width)
    w_gate_other = other_core(w_gate)
    w_up_other = other_core(w_up)
    query_rows_other = across(query_rows, 2)

    w_own = jnp.concatenate([w_gate, w_up], axis=1)
    partial = small_call(
        products_kernel, (chips * SLOTS, 4 * units), 4, rows, w_own, w_gate_other, w_up_other
    )
    share = chips * SLOTS // blocks
    partial, query_rows, query_rows_other = tie(partial, query_rows, query_rows_other)
    summed = exchange(partial.reshape(blocks, share, 4 * units), "z")
    hidden_copies = small_call(hidden_kernel, (blocks, share, 2 * units), 1, summed)
    query_rows = in_order(query_rows, query_rows_other, 2).reshape((-1,) + w_query.shape)
    w_query_full = lax.all_gather(query_rows, ("x", "core"), axis=0)
    w_query_full = w_query_full.reshape((-1, 2) + query_rows.shape)
    hidden = exchange(hidden_copies, "z").reshape(chips * SLOTS, 2 * units)
    w_down_other = other_core(w_down)
    out_part = jnp.dot(hidden[:, :units], w_down, preferred_element_type=jnp.float32) + jnp.dot(
        hidden[:, units:], w_down_other, preferred_element_type=jnp.float32
    )
    out_part = out_part.astype(jnp.bfloat16)
    pieces = exchange(out_part.reshape(chips, SLOTS, block_width), CHIPS)
    out_copies = small_call(total_kernel, (experts * blocks, PADDED, block_width), 1, pieces)
    table = exchange(out_copies, EXPERT).reshape(-1, block_width)

    column = jnp.where(served, expert_of * PADDED + slot_of, -1)
    return finish(tokens, table, column, gate_of, norm_gain, w_query_full)


def solution(mesh):
    fine = Mesh(mesh.devices.reshape(tuple(SIZES.values())), tuple(SIZES))
    in_specs = (
        P(DP, None),
        P(DP),
        P(DP),
        P(DP),
        P(DP),
        P(DP),
        P(DP),
        P(EXPERT, DP),
        P(EXPERT, DP),
        P(DP, EXPERT),
        P(),
        P(DP, EXPERT),
    )
    out_specs = (P(DP, None), P(DP, EXPERT))
    return jax.shard_map(local, mesh=fine, in_specs=in_specs, out_specs=out_specs, check_vma=False)
```

```python
import jax
import jax.numpy as jnp
from jax import lax
from jax.experimental import pallas as pl
from jax.experimental.pallas import tpu as pltpu
from jax.sharding import Mesh, PartitionSpec as P

CAP1 = 4
CAP2 = 2
SLOTS = CAP1 + CAP2
EXPERT = ("y_lo", "z")
CHIPS = ("y_hi", "x")
DP = ("y_hi", "x", "core")
SIZES = {"y_lo": 2, "z": 8, "y_hi": 4, "x": 8, "core": 2}
PADDED = 8
LANES = 128
VMEM_BYTES = 60 * 1024 * 1024
FINISH_BYTES = 50 * 1024 * 1024


def exchange(blocks, axes):
    return lax.all_to_all(blocks, axes, split_axis=0, concat_axis=0, tiled=True)


def other_core(block):
    return lax.ppermute(block, "core", [(0, 1), (1, 0)])


def across(block, bit):
    return lax.ppermute(block, "y_hi", [(i, i ^ bit) for i in range(lax.axis_size("y_hi"))])


def in_order(own, other, bit):
    upper = (lax.axis_index("y_hi") & bit) != 0
    return jnp.concatenate([jnp.where(upper, other, own), jnp.where(upper, own, other)], axis=0)


def tie(*values):
    return lax.optimization_barrier(values)


def small_call(kernel, shape, vmem_count, *operands, scratch=()):
    vmem = pl.BlockSpec(memory_space=pltpu.VMEM)
    outside = len(operands) - vmem_count
    size = 1
    for extent in shape:
        size *= extent
    return pl.pallas_call(
        kernel,
        out_shape=jax.ShapeDtypeStruct(shape, jnp.bfloat16),
        in_specs=[pl.BlockSpec(memory_space=pltpu.HBM)] * outside + [vmem] * vmem_count,
        out_specs=vmem,
        scratch_shapes=list(scratch),
        compiler_params=pltpu.CompilerParams(vmem_limit_bytes=VMEM_BYTES if outside else VMEM_BYTES // 4),
        cost_estimate=pl.CostEstimate(flops=2 * size, bytes_accessed=4 * size, transcendentals=0),
    )(*operands)


def slots_kernel(
    tokens_hbm, first_expert_ref, first_slot_ref, second_expert_ref, second_slot_ref, out_ref, block_ref, sem
):
    width = block_ref.shape[1]
    start = pl.multiple_of(lax.axis_index("z") * width, LANES)
    load = pltpu.make_async_copy(tokens_hbm.at[:, pl.ds(start, width)], block_ref, sem)
    load.start()
    own = lax.axis_index("y_lo")
    first, second = first_slot_ref[...], second_slot_ref[...]
    placement = jnp.where((second_expert_ref[...] == own) & (second >= 0), second + CAP1, -1)
    placement = jnp.where((first_expert_ref[...] == own) & (first >= 0), first, placement)
    slots = lax.broadcasted_iota(jnp.int32, (PADDED, placement.shape[1]), 0)
    hot = (slots == placement).astype(jnp.bfloat16)
    load.wait()
    rows = jnp.dot(hot, block_ref[...], preferred_element_type=jnp.float32).astype(jnp.bfloat16)
    for i in range(out_ref.shape[0]):
        out_ref[i] = rows[:SLOTS]


def products_kernel(rows_ref, own_ref, gate_other_ref, up_other_ref, out_ref):
    rows = rows_ref[...]
    units = gate_other_ref.shape[1]

    def product(at, w):
        out_ref[:, at * units : (at + 1) * units] = jnp.dot(
            rows, w, preferred_element_type=jnp.float32
        ).astype(jnp.bfloat16)

    product(0, own_ref[:, :units])
    product(1, gate_other_ref[...])
    product(2, own_ref[:, units:])
    product(3, up_other_ref[...])


def hidden_kernel(parts_ref, out_ref):
    units = out_ref.shape[2]
    total = parts_ref[0].astype(jnp.float32)
    for i in range(1, parts_ref.shape[0]):
        total += parts_ref[i].astype(jnp.float32)
    gate, up = total[:, :units], total[:, units:]
    hidden = (gate / (1.0 + jnp.exp(-gate)) * up).astype(jnp.bfloat16)
    for i in range(out_ref.shape[0]):
        out_ref[i] = hidden


def total_kernel(parts_ref, out_ref):
    total = parts_ref[0].astype(jnp.float32)
    for i in range(1, parts_ref.shape[0]):
        total += parts_ref[i].astype(jnp.float32)
    rows = jnp.concatenate([total, jnp.zeros((PADDED - SLOTS, total.shape[1]), jnp.float32)], axis=0)
    rows = rows.astype(jnp.bfloat16)
    for i in range(out_ref.shape[0]):
        out_ref[i] = rows


def finish_kernel(
    tokens_ref, table_ref, column_ref, gate_ref, gain_ref, w_hbm, mixed_ref, query_ref, normed_ref, w_ref, sem
):
    parts = w_ref.shape[0]
    loads = [pltpu.make_async_copy(w_hbm.at[i], w_ref.at[i], sem.at[i]) for i in range(parts)]
    for load in loads:
        load.start()
    blocks = table_ref.shape[0] // (2 * PADDED)
    tok_count, width = tokens_ref.shape
    block_width = width // blocks
    column = column_ref[...]
    slots = lax.broadcasted_iota(jnp.int32, (tok_count, PADDED), 1)
    hot = [(column == slots + e * PADDED).astype(jnp.bfloat16) for e in range(2)]
    gate = gate_ref[...]
    square = jnp.zeros((tok_count, LANES), jnp.float32)
    for z in range(blocks):
        cols = pl.ds(z * block_width, block_width)
        picked = sum(
            jnp.dot(
                hot[e],
                table_ref[pl.ds((e * blocks + z) * PADDED, PADDED), :],
                preferred_element_type=jnp.float32,
            )
            for e in range(2)
        )
        mixed = (tokens_ref[:, cols].astype(jnp.float32) + gate * picked).astype(jnp.bfloat16)
        mixed_ref[:, cols] = mixed
        values = mixed.astype(jnp.float32)
        for i in range(block_width // LANES):
            part = values[:, i * LANES : (i + 1) * LANES]
            square += part * part
    mean = jnp.sum(square, axis=1, keepdims=True) * (1.0 / width)
    scale = lax.rsqrt(mean + 1e-05)
    for z in range(blocks):
        cols = pl.ds(z * block_width, block_width)
        values = mixed_ref[:, cols].astype(jnp.float32)
        normed_ref[:, cols] = (values * scale * gain_ref[:, cols]).astype(jnp.bfloat16)
    cores, ys, rows = w_ref.shape[1:4]
    pair = 2 * cores * rows
    query = jnp.zeros(query_ref.shape, jnp.float32)
    for x in range(0, parts, 2):
        loads[x].wait()
        loads[x + 1].wait()
        for y in range(ys):
            block = jnp.concatenate([w_ref[x + i, c, y] for i in range(2) for c in range(cores)], axis=0)
            start = (y * parts + x) * cores * rows
            query += jnp.dot(
                normed_ref[:, start : start + pair], block, preferred_element_type=jnp.float32
            )
    query_ref[...] = query.astype(query_ref.dtype)


def finish(tokens, table, column, gate, gain, w_query):
    vmem = pl.BlockSpec(memory_space=pltpu.VMEM)
    tok_count, width = tokens.shape
    columns = w_query.shape[-1]
    return pl.pallas_call(
        finish_kernel,
        out_shape=(
            jax.ShapeDtypeStruct((tok_count, width), jnp.bfloat16),
            jax.ShapeDtypeStruct((tok_count, columns), jnp.bfloat16),
        ),
        in_specs=[vmem] * 5 + [pl.BlockSpec(memory_space=pltpu.HBM)],
        out_specs=(vmem, vmem),
        scratch_shapes=[
            pltpu.VMEM((tok_count, width), jnp.bfloat16),
            pltpu.VMEM(w_query.shape, jnp.bfloat16),
            pltpu.SemaphoreType.DMA((w_query.shape[0],)),
        ],
        compiler_params=pltpu.CompilerParams(vmem_limit_bytes=FINISH_BYTES),
        cost_estimate=pl.CostEstimate(
            flops=2 * tok_count * width * columns, bytes_accessed=4 * width * columns, transcendentals=0
        ),
    )(tokens, table, column[:, None], gate[:, None], gain[None, :], w_query)


def local(
    tokens,
    first_expert,
    first_slot,
    second_expert,
    second_slot,
    first_gate,
    second_gate,
    w_gate,
    w_up,
    w_down,
    norm_gain,
    w_query,
):
    tok_count, width = tokens.shape
    blocks = lax.axis_size("z")
    chips = lax.axis_size(CHIPS)
    block_width = width // blocks
    units = w_gate.shape[1]
    experts = lax.axis_size("y_lo")

    served_first = first_slot >= 0
    served = served_first | (second_slot >= 0)
    expert_of = jnp.where(served_first, first_expert, second_expert)
    slot_of = jnp.where(served_first, first_slot, second_slot + CAP1)
    gate_of = jnp.where(served_first, first_gate, second_gate)

    slot_copies = small_call(
        slots_kernel,
        (chips, SLOTS, block_width),
        4,
        tokens,
        first_expert[None, :],
        first_slot[None, :],
        second_expert[None, :],
        second_slot[None, :],
        scratch=(pltpu.VMEM((tok_count, block_width), jnp.bfloat16), pltpu.SemaphoreType.DMA(())),
    )
    slot_copies, w_query = tie(slot_copies, w_query)
    rows = exchange(slot_copies, CHIPS).reshape(chips * SLOTS, block_width)
    w_gate_other = other_core(w_gate)
    w_up_other = other_core(w_up)
    w_query_beside = across(w_query, 1)

    w_own = jnp.concatenate([w_gate, w_up], axis=1)
    partial = small_call(
        products_kernel, (chips * SLOTS, 4 * units), 4, rows, w_own, w_gate_other, w_up_other
    )
    share = chips * SLOTS // blocks
    partial, w_query, w_query_beside = tie(partial, w_query, w_query_beside)
    summed = exchange(partial.reshape(blocks, share, 4 * units), "z")
    query_rows = in_order(w_query, w_query_beside, 1)
    query_rows_other = across(query_rows, 2)
    hidden_copies = small_call(hidden_kernel, (blocks, share, 2 * units), 1, summed)
    hidden_copies, query_rows_other = tie(hidden_copies, query_rows_other)
    query_rows = in_order(query_rows, query_rows_other, 2).reshape((-1,) + w_query.shape)
    w_query_full = lax.all_gather(query_rows, ("x", "core"), axis=0)
    w_query_full = w_query_full.reshape((-1, 2) + query_rows.shape)
    hidden = exchange(hidden_copies, "z").reshape(chips * SLOTS, 2 * units)
    w_down_other = other_core(w_down)
    out_part = jnp.dot(hidden[:, :units], w_down, preferred_element_type=jnp.float32) + jnp.dot(
        hidden[:, units:], w_down_other, preferred_element_type=jnp.float32
    )
    out_part = out_part.astype(jnp.bfloat16)
    pieces = exchange(out_part.reshape(chips, SLOTS, block_width), CHIPS)
    out_copies = small_call(total_kernel, (experts * blocks, PADDED, block_width), 1, pieces)
    table = exchange(out_copies, EXPERT).reshape(-1, block_width)

    column = jnp.where(served, expert_of * PADDED + slot_of, -1)
    return finish(tokens, table, column, gate_of, norm_gain, w_query_full)


def solution(mesh):
    fine = Mesh(mesh.devices.reshape(tuple(SIZES.values())), tuple(SIZES))
    in_specs = (
        P(DP, None),
        P(DP),
        P(DP),
        P(DP),
        P(DP),
        P(DP),
        P(DP),
        P(EXPERT, DP),
        P(EXPERT, DP),
        P(DP, EXPERT),
        P(),
        P(DP, EXPERT),
    )
    out_specs = (P(DP, None), P(DP, EXPERT))
    return jax.shard_map(local, mesh=fine, in_specs=in_specs, out_specs=out_specs, check_vma=False)
```

```python
import jax
import jax.numpy as jnp
from jax import lax
from jax.experimental import pallas as pl
from jax.experimental.pallas import tpu as pltpu
from jax.sharding import Mesh, PartitionSpec as P

CAP1 = 4
CAP2 = 2
SLOTS = CAP1 + CAP2
EXPERT = ("y_lo", "z")
CHIPS = ("y_hi", "x")
DP = ("y_hi", "x", "core")
SIZES = {"y_lo": 2, "z": 8, "y_hi": 4, "x": 8, "core": 2}
PADDED = 8
LANES = 128
PIECES = 4
VMEM_BYTES = 60 * 1024 * 1024
FINISH_BYTES = 50 * 1024 * 1024


def exchange(blocks, axes):
    return lax.all_to_all(blocks, axes, split_axis=0, concat_axis=0, tiled=True)


def other_core(block):
    return lax.ppermute(block, "core", [(0, 1), (1, 0)])


def across(block, bit):
    return lax.ppermute(block, "y_hi", [(i, i ^ bit) for i in range(lax.axis_size("y_hi"))])


def in_order(own, other, bit, axis):
    upper = (lax.axis_index("y_hi") & bit) != 0
    return jnp.stack([jnp.where(upper, other, own), jnp.where(upper, own, other)], axis=axis)


def tie(*values):
    return lax.optimization_barrier(values)


def small_call(kernel, shape, vmem_count, *operands, scratch=()):
    vmem = pl.BlockSpec(memory_space=pltpu.VMEM)
    outside = len(operands) - vmem_count
    size = 1
    for extent in shape:
        size *= extent
    return pl.pallas_call(
        kernel,
        out_shape=jax.ShapeDtypeStruct(shape, jnp.bfloat16),
        in_specs=[pl.BlockSpec(memory_space=pltpu.HBM)] * outside + [vmem] * vmem_count,
        out_specs=vmem,
        scratch_shapes=list(scratch),
        compiler_params=pltpu.CompilerParams(vmem_limit_bytes=VMEM_BYTES if outside else VMEM_BYTES // 4),
        cost_estimate=pl.CostEstimate(flops=2 * size, bytes_accessed=4 * size, transcendentals=0),
    )(*operands)


def slots_kernel(
    tokens_hbm, first_expert_hbm, first_slot_hbm, second_expert_hbm, second_slot_hbm, out_ref, block_ref, *refs
):
    ids, sem = refs[:-1], refs[-1]
    width = block_ref.shape[1]
    start = pl.multiple_of(lax.axis_index("z") * width, LANES)
    sources = (first_expert_hbm, first_slot_hbm, second_expert_hbm, second_slot_hbm)
    loads = [pltpu.make_async_copy(s, d, sem.at[i]) for i, (s, d) in enumerate(zip(sources, ids, strict=True))]
    share = block_ref.shape[0] // PIECES
    for i in range(PIECES):
        rows = pl.ds(i * share, share)
        loads.append(
            pltpu.make_async_copy(
                tokens_hbm.at[rows, pl.ds(start, width)], block_ref.at[rows], sem.at[len(ids) + i]
            )
        )
    for load in loads:
        load.start()
    for load in loads[: len(ids)]:
        load.wait()
    own = lax.axis_index("y_lo")
    first_expert, first, second_expert, second = (ref[...] for ref in ids)
    placement = jnp.where((second_expert == own) & (second >= 0), second + CAP1, -1)
    placement = jnp.where((first_expert == own) & (first >= 0), first, placement)
    slots = lax.broadcasted_iota(jnp.int32, (PADDED, placement.shape[1]), 0)
    hot = (slots == placement).astype(jnp.bfloat16)
    for load in loads[len(ids) :]:
        load.wait()
    rows = jnp.dot(hot, block_ref[...], preferred_element_type=jnp.float32).astype(jnp.bfloat16)
    for i in range(out_ref.shape[0]):
        out_ref[i] = rows[:SLOTS]


def products_kernel(rows_ref, own_ref, gate_other_ref, up_other_ref, out_ref):
    rows = rows_ref[...]
    units = gate_other_ref.shape[1]

    def product(at, w):
        out_ref[:, at * units : (at + 1) * units] = jnp.dot(
            rows, w, preferred_element_type=jnp.float32
        ).astype(jnp.bfloat16)

    product(0, own_ref[:, :units])
    product(1, gate_other_ref[...])
    product(2, own_ref[:, units:])
    product(3, up_other_ref[...])


def hidden_kernel(parts_ref, out_ref):
    units = out_ref.shape[2]
    total = parts_ref[0].astype(jnp.float32)
    for i in range(1, parts_ref.shape[0]):
        total += parts_ref[i].astype(jnp.float32)
    gate, up = total[:, :units], total[:, units:]
    hidden = (gate / (1.0 + jnp.exp(-gate)) * up).astype(jnp.bfloat16)
    for i in range(out_ref.shape[0]):
        out_ref[i] = hidden


def total_kernel(parts_ref, out_ref):
    total = parts_ref[0].astype(jnp.float32)
    for i in range(1, parts_ref.shape[0]):
        total += parts_ref[i].astype(jnp.float32)
    rows = jnp.concatenate([total, jnp.zeros((PADDED - SLOTS, total.shape[1]), jnp.float32)], axis=0)
    rows = rows.astype(jnp.bfloat16)
    for i in range(out_ref.shape[0]):
        out_ref[i] = rows


def finish_kernel(
    tokens_ref, table_ref, column_ref, gate_ref, gain_ref, w_hbm, mixed_ref, query_ref, normed_ref, w_ref, sem
):
    parts = w_ref.shape[0]
    loads = [pltpu.make_async_copy(w_hbm.at[i], w_ref.at[i], sem.at[i]) for i in range(parts)]
    for load in loads:
        load.start()
    blocks = table_ref.shape[0] // (2 * PADDED)
    tok_count, width = tokens_ref.shape
    block_width = width // blocks
    column = column_ref[...]
    slots = lax.broadcasted_iota(jnp.int32, (tok_count, PADDED), 1)
    hot = [(column == slots + e * PADDED).astype(jnp.bfloat16) for e in range(2)]
    gate = gate_ref[...]
    square = jnp.zeros((tok_count, LANES), jnp.float32)
    for z in range(blocks):
        cols = pl.ds(z * block_width, block_width)
        picked = sum(
            jnp.dot(
                hot[e],
                table_ref[pl.ds((e * blocks + z) * PADDED, PADDED), :],
                preferred_element_type=jnp.float32,
            )
            for e in range(2)
        )
        mixed = (tokens_ref[:, cols].astype(jnp.float32) + gate * picked).astype(jnp.bfloat16)
        mixed_ref[:, cols] = mixed
        values = mixed.astype(jnp.float32)
        for i in range(block_width // LANES):
            part = values[:, i * LANES : (i + 1) * LANES]
            square += part * part
    mean = jnp.sum(square, axis=1, keepdims=True) * (1.0 / width)
    scale = lax.rsqrt(mean + 1e-05)
    for z in range(blocks):
        cols = pl.ds(z * block_width, block_width)
        values = mixed_ref[:, cols].astype(jnp.float32)
        normed_ref[:, cols] = (values * scale * gain_ref[:, cols]).astype(jnp.bfloat16)
    cores, ys, rows = w_ref.shape[1:4]
    pair = 2 * cores * rows
    query = jnp.zeros(query_ref.shape, jnp.float32)
    for x in range(0, parts, 2):
        loads[x].wait()
        loads[x + 1].wait()
        for y in range(ys):
            block = jnp.concatenate([w_ref[x + i, c, y] for i in range(2) for c in range(cores)], axis=0)
            start = (y * parts + x) * cores * rows
            query += jnp.dot(
                normed_ref[:, start : start + pair], block, preferred_element_type=jnp.float32
            )
    query_ref[...] = query.astype(query_ref.dtype)


def finish(tokens, table, column, gate, gain, w_query):
    vmem = pl.BlockSpec(memory_space=pltpu.VMEM)
    tok_count, width = tokens.shape
    columns = w_query.shape[-1]
    return pl.pallas_call(
        finish_kernel,
        out_shape=(
            jax.ShapeDtypeStruct((tok_count, width), jnp.bfloat16),
            jax.ShapeDtypeStruct((tok_count, columns), jnp.bfloat16),
        ),
        in_specs=[vmem] * 5 + [pl.BlockSpec(memory_space=pltpu.HBM)],
        out_specs=(vmem, vmem),
        scratch_shapes=[
            pltpu.VMEM((tok_count, width), jnp.bfloat16),
            pltpu.VMEM(w_query.shape, jnp.bfloat16),
            pltpu.SemaphoreType.DMA((w_query.shape[0],)),
        ],
        compiler_params=pltpu.CompilerParams(vmem_limit_bytes=FINISH_BYTES),
        cost_estimate=pl.CostEstimate(
            flops=2 * tok_count * width * columns, bytes_accessed=4 * width * columns, transcendentals=0
        ),
    )(tokens, table, column[:, None], gate[:, None], gain[None, :], w_query)


def local(
    tokens,
    first_expert,
    first_slot,
    second_expert,
    second_slot,
    first_gate,
    second_gate,
    w_gate,
    w_up,
    w_down,
    norm_gain,
    w_query,
):
    tok_count, width = tokens.shape
    blocks = lax.axis_size("z")
    chips = lax.axis_size(CHIPS)
    block_width = width // blocks
    units = w_gate.shape[1]
    experts = lax.axis_size("y_lo")

    served_first = first_slot >= 0
    served = served_first | (second_slot >= 0)
    expert_of = jnp.where(served_first, first_expert, second_expert)
    slot_of = jnp.where(served_first, first_slot, second_slot + CAP1)
    gate_of = jnp.where(served_first, first_gate, second_gate)

    slot_copies = small_call(
        slots_kernel,
        (chips, SLOTS, block_width),
        0,
        tokens,
        first_expert[None, :],
        first_slot[None, :],
        second_expert[None, :],
        second_slot[None, :],
        scratch=(
            pltpu.VMEM((tok_count, block_width), jnp.bfloat16),
            *[pltpu.VMEM((1, tok_count), jnp.int32)] * 4,
            pltpu.SemaphoreType.DMA((4 + PIECES,)),
        ),
    )
    slot_copies, w_query = tie(slot_copies, w_query)
    rows = exchange(slot_copies, CHIPS).reshape(chips * SLOTS, block_width)
    w_gate_other = other_core(w_gate)
    w_up_other = other_core(w_up)
    w_query_beside = across(w_query, 2)

    w_own = jnp.concatenate([w_gate, w_up], axis=1)
    partial = small_call(
        products_kernel, (chips * SLOTS, 4 * units), 4, rows, w_own, w_gate_other, w_up_other
    )
    share = chips * SLOTS // blocks
    partial, w_query, w_query_beside = tie(partial, w_query, w_query_beside)
    summed = exchange(partial.reshape(blocks, share, 4 * units), "z")
    query_rows = in_order(w_query, w_query_beside, 2, 0)
    query_rows_other = across(query_rows, 1)
    hidden_copies = small_call(hidden_kernel, (blocks, share, 2 * units), 1, summed)
    hidden_copies, query_rows_other = tie(hidden_copies, query_rows_other)
    query_rows = in_order(query_rows, query_rows_other, 1, 1).reshape((-1,) + w_query.shape)
    w_query_full = lax.all_gather(query_rows, ("x", "core"), axis=0)
    w_query_full = w_query_full.reshape((-1, 2) + query_rows.shape)
    hidden = exchange(hidden_copies, "z").reshape(chips * SLOTS, 2 * units)
    w_down_other = other_core(w_down)
    out_part = jnp.dot(hidden[:, :units], w_down, preferred_element_type=jnp.float32) + jnp.dot(
        hidden[:, units:], w_down_other, preferred_element_type=jnp.float32
    )
    out_part = out_part.astype(jnp.bfloat16)
    pieces = exchange(out_part.reshape(chips, SLOTS, block_width), CHIPS)
    out_copies = small_call(total_kernel, (experts * blocks, PADDED, block_width), 1, pieces)
    table = exchange(out_copies, EXPERT).reshape(-1, block_width)

    column = jnp.where(served, expert_of * PADDED + slot_of, -1)
    return finish(tokens, table, column, gate_of, norm_gain, w_query_full)


def solution(mesh):
    fine = Mesh(mesh.devices.reshape(tuple(SIZES.values())), tuple(SIZES))
    in_specs = (
        P(DP, None),
        P(DP),
        P(DP),
        P(DP),
        P(DP),
        P(DP),
        P(DP),
        P(EXPERT, DP),
        P(EXPERT, DP),
        P(DP, EXPERT),
        P(),
        P(DP, EXPERT),
    )
    out_specs = (P(DP, None), P(DP, EXPERT))
    return jax.shard_map(local, mesh=fine, in_specs=in_specs, out_specs=out_specs, check_vma=False)
```

```python
import jax
import jax.numpy as jnp
from jax import lax
from jax.experimental import pallas as pl
from jax.experimental.pallas import tpu as pltpu
from jax.sharding import Mesh, PartitionSpec as P

CAP1 = 4
CAP2 = 2
SLOTS = CAP1 + CAP2
EXPERT = ("y_lo", "z")
CHIPS = ("y_hi", "x")
DP = ("y_hi", "x", "core")
SIZES = {"y_lo": 2, "z": 8, "y_hi": 4, "x": 8, "core": 2}
PADDED = 8
LANES = 128
PIECES = 4
VMEM_BYTES = 60 * 1024 * 1024
FINISH_BYTES = 50 * 1024 * 1024


def exchange(blocks, axes):
    return lax.all_to_all(blocks, axes, split_axis=0, concat_axis=0, tiled=True)


def other_core(block):
    return lax.ppermute(block, "core", [(0, 1), (1, 0)])


def across(block, bit):
    return lax.ppermute(block, "y_hi", [(i, i ^ bit) for i in range(lax.axis_size("y_hi"))])


def in_order(own, other, bit, axis):
    upper = (lax.axis_index("y_hi") & bit) != 0
    return jnp.stack([jnp.where(upper, other, own), jnp.where(upper, own, other)], axis=axis)


def tie(*values):
    return lax.optimization_barrier(values)


def small_call(kernel, shape, vmem_count, *operands, scratch=()):
    vmem = pl.BlockSpec(memory_space=pltpu.VMEM)
    outside = len(operands) - vmem_count
    size = 1
    for extent in shape:
        size *= extent
    return pl.pallas_call(
        kernel,
        out_shape=jax.ShapeDtypeStruct(shape, jnp.bfloat16),
        in_specs=[pl.BlockSpec(memory_space=pltpu.HBM)] * outside + [vmem] * vmem_count,
        out_specs=vmem,
        scratch_shapes=list(scratch),
        compiler_params=pltpu.CompilerParams(vmem_limit_bytes=VMEM_BYTES if outside else VMEM_BYTES // 4),
        cost_estimate=pl.CostEstimate(flops=2 * size, bytes_accessed=4 * size, transcendentals=0),
    )(*operands)


def slots_kernel(
    tokens_hbm, first_expert_hbm, first_slot_hbm, second_expert_hbm, second_slot_hbm, out_ref, block_ref, *refs
):
    ids, sem = refs[:-1], refs[-1]
    width = block_ref.shape[1]
    start = pl.multiple_of(lax.axis_index("z") * width, LANES)
    sources = (first_expert_hbm, first_slot_hbm, second_expert_hbm, second_slot_hbm)
    loads = [pltpu.make_async_copy(s, d, sem.at[i]) for i, (s, d) in enumerate(zip(sources, ids, strict=True))]
    share = block_ref.shape[0] // PIECES
    for i in range(PIECES):
        rows = pl.ds(i * share, share)
        loads.append(
            pltpu.make_async_copy(
                tokens_hbm.at[rows, pl.ds(start, width)], block_ref.at[rows], sem.at[len(ids) + i]
            )
        )
    for load in loads:
        load.start()
    for load in loads[: len(ids)]:
        load.wait()
    own = lax.axis_index("y_lo")
    first_expert, first, second_expert, second = (ref[...] for ref in ids)
    placement = jnp.where((second_expert == own) & (second >= 0), second + CAP1, -1)
    placement = jnp.where((first_expert == own) & (first >= 0), first, placement)
    slots = lax.broadcasted_iota(jnp.int32, (PADDED, placement.shape[1]), 0)
    hot = (slots == placement).astype(jnp.bfloat16)
    for load in loads[len(ids) :]:
        load.wait()
    rows = jnp.dot(hot, block_ref[...], preferred_element_type=jnp.float32).astype(jnp.bfloat16)
    for i in range(out_ref.shape[0]):
        out_ref[i] = rows[:SLOTS]


def products_kernel(rows_ref, own_ref, gate_other_ref, up_other_ref, out_ref):
    rows = rows_ref[...]
    units = gate_other_ref.shape[1]

    def product(at, w):
        out_ref[:, at * units : (at + 1) * units] = jnp.dot(
            rows, w, preferred_element_type=jnp.float32
        ).astype(jnp.bfloat16)

    product(0, own_ref[:, :units])
    product(1, gate_other_ref[...])
    product(2, own_ref[:, units:])
    product(3, up_other_ref[...])


def hidden_kernel(parts_ref, out_ref):
    units = out_ref.shape[2]
    total = parts_ref[0].astype(jnp.float32)
    for i in range(1, parts_ref.shape[0]):
        total += parts_ref[i].astype(jnp.float32)
    gate, up = total[:, :units], total[:, units:]
    hidden = (gate / (1.0 + jnp.exp(-gate)) * up).astype(jnp.bfloat16)
    for i in range(out_ref.shape[0]):
        out_ref[i] = hidden


def total_kernel(parts_ref, out_ref):
    total = parts_ref[0].astype(jnp.float32)
    for i in range(1, parts_ref.shape[0]):
        total += parts_ref[i].astype(jnp.float32)
    rows = jnp.concatenate([total, jnp.zeros((PADDED - SLOTS, total.shape[1]), jnp.float32)], axis=0)
    rows = rows.astype(jnp.bfloat16)
    for i in range(out_ref.shape[0]):
        out_ref[i] = rows


def finish_kernel(
    tokens_ref, table_ref, column_ref, gate_ref, gain_ref, w_hbm, mixed_ref, query_ref, normed_ref, w_ref, sem
):
    parts = w_ref.shape[0]
    loads = [pltpu.make_async_copy(w_hbm.at[i], w_ref.at[i], sem.at[i]) for i in range(parts)]
    for load in loads:
        load.start()
    blocks = table_ref.shape[0] // (2 * PADDED)
    tok_count, width = tokens_ref.shape
    block_width = width // blocks
    column = column_ref[...]
    slots = lax.broadcasted_iota(jnp.int32, (tok_count, PADDED), 1)
    hot = [(column == slots + e * PADDED).astype(jnp.bfloat16) for e in range(2)]
    gate = gate_ref[...]
    square = jnp.zeros((tok_count, LANES), jnp.float32)
    for z in range(blocks):
        cols = pl.ds(z * block_width, block_width)
        picked = sum(
            jnp.dot(
                hot[e],
                table_ref[pl.ds((e * blocks + z) * PADDED, PADDED), :],
                preferred_element_type=jnp.float32,
            )
            for e in range(2)
        )
        mixed = (tokens_ref[:, cols].astype(jnp.float32) + gate * picked).astype(jnp.bfloat16)
        mixed_ref[:, cols] = mixed
        values = mixed.astype(jnp.float32)
        for i in range(block_width // LANES):
            part = values[:, i * LANES : (i + 1) * LANES]
            square += part * part
    mean = jnp.sum(square, axis=1, keepdims=True) * (1.0 / width)
    scale = lax.rsqrt(mean + 1e-05)
    for z in range(blocks):
        cols = pl.ds(z * block_width, block_width)
        values = mixed_ref[:, cols].astype(jnp.float32)
        normed_ref[:, cols] = (values * scale * gain_ref[:, cols]).astype(jnp.bfloat16)
    cores, ys, rows = w_ref.shape[1:4]
    pair = 2 * cores * rows
    query = jnp.zeros(query_ref.shape, jnp.float32)
    for x in range(0, parts, 2):
        loads[x].wait()
        loads[x + 1].wait()
        for y in range(ys):
            block = jnp.concatenate([w_ref[x + i, c, y] for i in range(2) for c in range(cores)], axis=0)
            start = (y * parts + x) * cores * rows
            query += jnp.dot(
                normed_ref[:, start : start + pair], block, preferred_element_type=jnp.float32
            )
    query_ref[...] = query.astype(query_ref.dtype)


def finish(tokens, table, column, gate, gain, w_query):
    vmem = pl.BlockSpec(memory_space=pltpu.VMEM)
    tok_count, width = tokens.shape
    columns = w_query.shape[-1]
    return pl.pallas_call(
        finish_kernel,
        out_shape=(
            jax.ShapeDtypeStruct((tok_count, width), jnp.bfloat16),
            jax.ShapeDtypeStruct((tok_count, columns), jnp.bfloat16),
        ),
        in_specs=[vmem] * 5 + [pl.BlockSpec(memory_space=pltpu.HBM)],
        out_specs=(vmem, vmem),
        scratch_shapes=[
            pltpu.VMEM((tok_count, width), jnp.bfloat16),
            pltpu.VMEM(w_query.shape, jnp.bfloat16),
            pltpu.SemaphoreType.DMA((w_query.shape[0],)),
        ],
        compiler_params=pltpu.CompilerParams(vmem_limit_bytes=FINISH_BYTES),
        cost_estimate=pl.CostEstimate(
            flops=2 * tok_count * width * columns, bytes_accessed=4 * width * columns, transcendentals=0
        ),
    )(tokens, table, column[:, None], gate[:, None], gain[None, :], w_query)


def local(
    tokens,
    first_expert,
    first_slot,
    second_expert,
    second_slot,
    first_gate,
    second_gate,
    w_gate,
    w_up,
    w_down,
    norm_gain,
    w_query,
):
    tok_count, width = tokens.shape
    blocks = lax.axis_size("z")
    chips = lax.axis_size(CHIPS)
    block_width = width // blocks
    units = w_gate.shape[1]
    experts = lax.axis_size("y_lo")

    served_first = first_slot >= 0
    served = served_first | (second_slot >= 0)
    expert_of = jnp.where(served_first, first_expert, second_expert)
    slot_of = jnp.where(served_first, first_slot, second_slot + CAP1)
    gate_of = jnp.where(served_first, first_gate, second_gate)

    slot_copies = small_call(
        slots_kernel,
        (chips, SLOTS, block_width),
        0,
        tokens,
        first_expert[None, :],
        first_slot[None, :],
        second_expert[None, :],
        second_slot[None, :],
        scratch=(
            pltpu.VMEM((tok_count, block_width), jnp.bfloat16),
            *[pltpu.VMEM((1, tok_count), jnp.int32)] * 4,
            pltpu.SemaphoreType.DMA((4 + PIECES,)),
        ),
    )
    slot_copies, w_query = tie(slot_copies, w_query)
    rows = exchange(slot_copies, CHIPS).reshape(chips * SLOTS, block_width)
    w_gate_other = other_core(w_gate)
    w_up_other = other_core(w_up)
    w_query_beside = across(w_query, 2)

    w_own = jnp.concatenate([w_gate, w_up], axis=1)
    partial = small_call(
        products_kernel, (chips * SLOTS, 4 * units), 4, rows, w_own, w_gate_other, w_up_other
    )
    share = chips * SLOTS // blocks
    _, w_query, w_query_beside = tie(partial, w_query, w_query_beside)
    summed = exchange(partial.reshape(blocks, share, 4 * units), "z")
    query_rows = in_order(w_query, w_query_beside, 2, 0)
    query_rows_other = across(query_rows, 1)
    hidden_copies = small_call(hidden_kernel, (blocks, share, 2 * units), 1, summed)
    hidden_copies, query_rows_other = tie(hidden_copies, query_rows_other)
    query_rows = in_order(query_rows, query_rows_other, 1, 1).reshape((-1,) + w_query.shape)
    w_query_full = lax.all_gather(query_rows, ("x", "core"), axis=0)
    w_query_full = w_query_full.reshape((-1, 2) + query_rows.shape)
    hidden = exchange(hidden_copies, "z").reshape(chips * SLOTS, 2 * units)
    w_down_other = other_core(w_down)
    out_part = jnp.dot(hidden[:, :units], w_down, preferred_element_type=jnp.float32) + jnp.dot(
        hidden[:, units:], w_down_other, preferred_element_type=jnp.float32
    )
    out_part = out_part.astype(jnp.bfloat16)
    pieces = exchange(out_part.reshape(chips, SLOTS, block_width), CHIPS)
    out_copies = small_call(total_kernel, (experts * blocks, PADDED, block_width), 1, pieces)
    table = exchange(out_copies, EXPERT).reshape(-1, block_width)

    column = jnp.where(served, expert_of * PADDED + slot_of, -1)
    return finish(tokens, table, column, gate_of, norm_gain, w_query_full)


def solution(mesh):
    fine = Mesh(mesh.devices.reshape(tuple(SIZES.values())), tuple(SIZES))
    in_specs = (
        P(DP, None),
        P(DP),
        P(DP),
        P(DP),
        P(DP),
        P(DP),
        P(DP),
        P(EXPERT, DP),
        P(EXPERT, DP),
        P(DP, EXPERT),
        P(),
        P(DP, EXPERT),
    )
    out_specs = (P(DP, None), P(DP, EXPERT))
    return jax.shard_map(local, mesh=fine, in_specs=in_specs, out_specs=out_specs, check_vma=False)
```

```python
import jax
import jax.numpy as jnp
from jax import lax
from jax.experimental import pallas as pl
from jax.experimental.pallas import tpu as pltpu
from jax.sharding import Mesh, PartitionSpec as P

CAP1 = 4
CAP2 = 2
SLOTS = CAP1 + CAP2
EXPERT = ("y_lo", "z")
CHIPS = ("y_hi", "x")
DP = ("y_hi", "x", "core")
SIZES = {"y_lo": 2, "z": 8, "y_hi": 4, "x": 8, "core": 2}
PADDED = 8
LANES = 128
PIECES = 4
VMEM_BYTES = 60 * 1024 * 1024
FINISH_BYTES = 50 * 1024 * 1024


def exchange(blocks, axes):
    return lax.all_to_all(blocks, axes, split_axis=0, concat_axis=0, tiled=True)


def other_core(block):
    return lax.ppermute(block, "core", [(0, 1), (1, 0)])


def across(block, bit):
    return lax.ppermute(block, "y_hi", [(i, i ^ bit) for i in range(lax.axis_size("y_hi"))])


def in_order(own, other, bit, axis):
    upper = (lax.axis_index("y_hi") & bit) != 0
    return jnp.stack([jnp.where(upper, other, own), jnp.where(upper, own, other)], axis=axis)


def tie(*values):
    return lax.optimization_barrier(values)


def small_call(kernel, shape, vmem_count, *operands, scratch=()):
    vmem = pl.BlockSpec(memory_space=pltpu.VMEM)
    outside = len(operands) - vmem_count
    size = 1
    for extent in shape:
        size *= extent
    return pl.pallas_call(
        kernel,
        out_shape=jax.ShapeDtypeStruct(shape, jnp.bfloat16),
        in_specs=[pl.BlockSpec(memory_space=pltpu.HBM)] * outside + [vmem] * vmem_count,
        out_specs=vmem,
        scratch_shapes=list(scratch),
        compiler_params=pltpu.CompilerParams(vmem_limit_bytes=VMEM_BYTES if outside else VMEM_BYTES // 4),
        cost_estimate=pl.CostEstimate(flops=2 * size, bytes_accessed=4 * size, transcendentals=0),
    )(*operands)


def slots_kernel(
    tokens_hbm, first_expert_hbm, first_slot_hbm, second_expert_hbm, second_slot_hbm, out_ref, block_ref, *refs
):
    ids, sem = refs[:-1], refs[-1]
    width = block_ref.shape[1]
    start = pl.multiple_of(lax.axis_index("z") * width, LANES)
    sources = (first_expert_hbm, first_slot_hbm, second_expert_hbm, second_slot_hbm)
    loads = [pltpu.make_async_copy(s, d, sem.at[i]) for i, (s, d) in enumerate(zip(sources, ids, strict=True))]
    share = block_ref.shape[0] // PIECES
    for i in range(PIECES):
        rows = pl.ds(i * share, share)
        loads.append(
            pltpu.make_async_copy(
                tokens_hbm.at[rows, pl.ds(start, width)], block_ref.at[rows], sem.at[len(ids) + i]
            )
        )
    for load in loads:
        load.start()
    for load in loads[: len(ids)]:
        load.wait()
    own = lax.axis_index("y_lo")
    first_expert, first, second_expert, second = (ref[...] for ref in ids)
    placement = jnp.where((second_expert == own) & (second >= 0), second + CAP1, -1)
    placement = jnp.where((first_expert == own) & (first >= 0), first, placement)
    slots = lax.broadcasted_iota(jnp.int32, (PADDED, placement.shape[1]), 0)
    hot = (slots == placement).astype(jnp.bfloat16)
    for load in loads[len(ids) :]:
        load.wait()
    rows = jnp.dot(hot, block_ref[...], preferred_element_type=jnp.float32).astype(jnp.bfloat16)
    for i in range(out_ref.shape[0]):
        out_ref[i] = rows[:SLOTS]


def products_kernel(rows_ref, own_ref, gate_other_ref, up_other_ref, out_ref):
    rows = rows_ref[...]
    units = gate_other_ref.shape[1]

    def product(at, w):
        out_ref[:, at * units : (at + 1) * units] = jnp.dot(
            rows, w, preferred_element_type=jnp.float32
        ).astype(jnp.bfloat16)

    product(0, own_ref[:, :units])
    product(1, gate_other_ref[...])
    product(2, own_ref[:, units:])
    product(3, up_other_ref[...])


def hidden_kernel(parts_ref, out_ref):
    units = out_ref.shape[2]
    total = parts_ref[0].astype(jnp.float32)
    for i in range(1, parts_ref.shape[0]):
        total += parts_ref[i].astype(jnp.float32)
    gate, up = total[:, :units], total[:, units:]
    hidden = (gate / (1.0 + jnp.exp(-gate)) * up).astype(jnp.bfloat16)
    for i in range(out_ref.shape[0]):
        out_ref[i] = hidden


def total_kernel(parts_ref, out_ref):
    total = parts_ref[0].astype(jnp.float32)
    for i in range(1, parts_ref.shape[0]):
        total += parts_ref[i].astype(jnp.float32)
    rows = jnp.concatenate([total, jnp.zeros((PADDED - SLOTS, total.shape[1]), jnp.float32)], axis=0)
    rows = rows.astype(jnp.bfloat16)
    for i in range(out_ref.shape[0]):
        out_ref[i] = rows


def finish_kernel(
    tokens_ref, table_ref, column_ref, gate_ref, gain_ref, w_hbm, mixed_ref, query_ref, normed_ref, w_ref, sem
):
    parts = w_ref.shape[0]
    loads = [pltpu.make_async_copy(w_hbm.at[i], w_ref.at[i], sem.at[i]) for i in range(parts)]
    for load in loads:
        load.start()
    blocks = table_ref.shape[0] // (2 * PADDED)
    tok_count, width = tokens_ref.shape
    block_width = width // blocks
    column = column_ref[...]
    slots = lax.broadcasted_iota(jnp.int32, (tok_count, PADDED), 1)
    hot = [(column == slots + e * PADDED).astype(jnp.bfloat16) for e in range(2)]
    gate = gate_ref[...]
    square = jnp.zeros((tok_count, LANES), jnp.float32)
    for z in range(blocks):
        cols = pl.ds(z * block_width, block_width)
        picked = sum(
            jnp.dot(
                hot[e],
                table_ref[pl.ds((e * blocks + z) * PADDED, PADDED), :],
                preferred_element_type=jnp.float32,
            )
            for e in range(2)
        )
        mixed = (tokens_ref[:, cols].astype(jnp.float32) + gate * picked).astype(jnp.bfloat16)
        mixed_ref[:, cols] = mixed
        values = mixed.astype(jnp.float32)
        for i in range(block_width // LANES):
            part = values[:, i * LANES : (i + 1) * LANES]
            square += part * part
    mean = jnp.sum(square, axis=1, keepdims=True) * (1.0 / width)
    scale = lax.rsqrt(mean + 1e-05)
    for z in range(blocks):
        cols = pl.ds(z * block_width, block_width)
        values = mixed_ref[:, cols].astype(jnp.float32)
        normed_ref[:, cols] = (values * scale * gain_ref[:, cols]).astype(jnp.bfloat16)
    cores, ys, rows = w_ref.shape[1:4]
    pair = 2 * cores * rows
    query = jnp.zeros(query_ref.shape, jnp.float32)
    for x in range(0, parts, 2):
        loads[x].wait()
        loads[x + 1].wait()
        for y in range(ys):
            block = jnp.concatenate([w_ref[x + i, c, y] for i in range(2) for c in range(cores)], axis=0)
            start = (y * parts + x) * cores * rows
            query += jnp.dot(
                normed_ref[:, start : start + pair], block, preferred_element_type=jnp.float32
            )
    query_ref[...] = query.astype(query_ref.dtype)


def finish(tokens, table, column, gate, gain, w_query):
    vmem = pl.BlockSpec(memory_space=pltpu.VMEM)
    tok_count, width = tokens.shape
    columns = w_query.shape[-1]
    return pl.pallas_call(
        finish_kernel,
        out_shape=(
            jax.ShapeDtypeStruct((tok_count, width), jnp.bfloat16),
            jax.ShapeDtypeStruct((tok_count, columns), jnp.bfloat16),
        ),
        in_specs=[vmem] * 5 + [pl.BlockSpec(memory_space=pltpu.HBM)],
        out_specs=(vmem, vmem),
        scratch_shapes=[
            pltpu.VMEM((tok_count, width), jnp.bfloat16),
            pltpu.VMEM(w_query.shape, jnp.bfloat16),
            pltpu.SemaphoreType.DMA((w_query.shape[0],)),
        ],
        compiler_params=pltpu.CompilerParams(vmem_limit_bytes=FINISH_BYTES),
        cost_estimate=pl.CostEstimate(
            flops=2 * tok_count * width * columns, bytes_accessed=4 * width * columns, transcendentals=0
        ),
    )(tokens, table, column[:, None], gate[:, None], gain[None, :], w_query)


def local(
    tokens,
    first_expert,
    first_slot,
    second_expert,
    second_slot,
    first_gate,
    second_gate,
    w_gate,
    w_up,
    w_down,
    norm_gain,
    w_query,
):
    tok_count, width = tokens.shape
    blocks = lax.axis_size("z")
    chips = lax.axis_size(CHIPS)
    block_width = width // blocks
    units = w_gate.shape[1]
    experts = lax.axis_size("y_lo")

    served_first = first_slot >= 0
    served = served_first | (second_slot >= 0)
    expert_of = jnp.where(served_first, first_expert, second_expert)
    slot_of = jnp.where(served_first, first_slot, second_slot + CAP1)
    gate_of = jnp.where(served_first, first_gate, second_gate)

    slot_copies = small_call(
        slots_kernel,
        (chips, SLOTS, block_width),
        0,
        tokens,
        first_expert[None, :],
        first_slot[None, :],
        second_expert[None, :],
        second_slot[None, :],
        scratch=(
            pltpu.VMEM((tok_count, block_width), jnp.bfloat16),
            *[pltpu.VMEM((1, tok_count), jnp.int32)] * 4,
            pltpu.SemaphoreType.DMA((4 + PIECES,)),
        ),
    )
    slot_copies, w_query = tie(slot_copies, w_query)
    rows = exchange(slot_copies, CHIPS).reshape(chips * SLOTS, block_width)
    w_gate_other = other_core(w_gate)
    w_up_other = other_core(w_up)
    w_query_beside = across(w_query, 1)

    w_own = jnp.concatenate([w_gate, w_up], axis=1)
    partial = small_call(
        products_kernel, (chips * SLOTS, 4 * units), 4, rows, w_own, w_gate_other, w_up_other
    )
    share = chips * SLOTS // blocks
    partial, w_query, w_query_beside = tie(partial, w_query, w_query_beside)
    summed = exchange(partial.reshape(blocks, share, 4 * units), "z")
    query_rows = in_order(w_query, w_query_beside, 1, 0)
    query_rows_other = across(query_rows, 2)
    hidden_copies = small_call(hidden_kernel, (blocks, share, 2 * units), 1, summed)
    hidden_copies, query_rows_other = tie(hidden_copies, query_rows_other)
    query_rows = in_order(query_rows, query_rows_other, 2, 0).reshape((-1,) + w_query.shape)
    w_query_full = lax.all_gather(query_rows, ("x", "core"), axis=0)
    w_query_full = w_query_full.reshape((-1, 2) + query_rows.shape)
    hidden = exchange(hidden_copies, "z").reshape(chips * SLOTS, 2 * units)
    w_down_other = other_core(w_down)
    out_part = jnp.dot(hidden[:, :units], w_down, preferred_element_type=jnp.float32) + jnp.dot(
        hidden[:, units:], w_down_other, preferred_element_type=jnp.float32
    )
    out_part = out_part.astype(jnp.bfloat16)
    pieces = exchange(out_part.reshape(chips, SLOTS, block_width), CHIPS)
    out_copies = small_call(total_kernel, (experts * blocks, PADDED, block_width), 1, pieces)
    table = exchange(out_copies, EXPERT).reshape(-1, block_width)

    column = jnp.where(served, expert_of * PADDED + slot_of, -1)
    return finish(tokens, table, column, gate_of, norm_gain, w_query_full)


def solution(mesh):
    fine = Mesh(mesh.devices.reshape(tuple(SIZES.values())), tuple(SIZES))
    in_specs = (
        P(DP, None),
        P(DP),
        P(DP),
        P(DP),
        P(DP),
        P(DP),
        P(DP),
        P(EXPERT, DP),
        P(EXPERT, DP),
        P(DP, EXPERT),
        P(),
        P(DP, EXPERT),
    )
    out_specs = (P(DP, None), P(DP, EXPERT))
    return jax.shard_map(local, mesh=fine, in_specs=in_specs, out_specs=out_specs, check_vma=False)
```

```python
import jax
import jax.numpy as jnp
from jax import lax
from jax.experimental import pallas as pl
from jax.experimental.pallas import tpu as pltpu
from jax.sharding import Mesh, PartitionSpec as P

CAP1 = 4
CAP2 = 2
SLOTS = CAP1 + CAP2
EXPERT = ("y_lo", "z")
CHIPS = ("y_hi", "x")
DP = ("y_hi", "x", "core")
SIZES = {"y_lo": 2, "z": 8, "y_hi": 4, "x": 8, "core": 2}
PADDED = 8
LANES = 128
PIECES = 8
VMEM_BYTES = 60 * 1024 * 1024
FINISH_BYTES = 50 * 1024 * 1024


def exchange(blocks, axes):
    return lax.all_to_all(blocks, axes, split_axis=0, concat_axis=0, tiled=True)


def other_core(block):
    return lax.ppermute(block, "core", [(0, 1), (1, 0)])


def across(block, bit):
    return lax.ppermute(block, "y_hi", [(i, i ^ bit) for i in range(lax.axis_size("y_hi"))])


def in_order(own, other, bit, axis):
    upper = (lax.axis_index("y_hi") & bit) != 0
    return jnp.stack([jnp.where(upper, other, own), jnp.where(upper, own, other)], axis=axis)


def tie(*values):
    return lax.optimization_barrier(values)


def small_call(kernel, shape, vmem_count, *operands, scratch=()):
    vmem = pl.BlockSpec(memory_space=pltpu.VMEM)
    outside = len(operands) - vmem_count
    size = 1
    for extent in shape:
        size *= extent
    return pl.pallas_call(
        kernel,
        out_shape=jax.ShapeDtypeStruct(shape, jnp.bfloat16),
        in_specs=[pl.BlockSpec(memory_space=pltpu.HBM)] * outside + [vmem] * vmem_count,
        out_specs=vmem,
        scratch_shapes=list(scratch),
        compiler_params=pltpu.CompilerParams(vmem_limit_bytes=VMEM_BYTES if outside else VMEM_BYTES // 4),
        cost_estimate=pl.CostEstimate(flops=2 * size, bytes_accessed=4 * size, transcendentals=0),
    )(*operands)


def slots_kernel(
    tokens_hbm, first_expert_hbm, first_slot_hbm, second_expert_hbm, second_slot_hbm, out_ref, block_ref, *refs
):
    ids, sem = refs[:-1], refs[-1]
    width = block_ref.shape[1]
    start = pl.multiple_of(lax.axis_index("z") * width, LANES)
    sources = (first_expert_hbm, first_slot_hbm, second_expert_hbm, second_slot_hbm)
    loads = [pltpu.make_async_copy(s, d, sem.at[i]) for i, (s, d) in enumerate(zip(sources, ids, strict=True))]
    share = block_ref.shape[0] // PIECES
    for i in range(PIECES):
        rows = pl.ds(i * share, share)
        loads.append(
            pltpu.make_async_copy(
                tokens_hbm.at[rows, pl.ds(start, width)], block_ref.at[rows], sem.at[len(ids) + i]
            )
        )
    for load in loads:
        load.start()
    for load in loads[: len(ids)]:
        load.wait()
    own = lax.axis_index("y_lo")
    first_expert, first, second_expert, second = (ref[...] for ref in ids)
    placement = jnp.where((second_expert == own) & (second >= 0), second + CAP1, -1)
    placement = jnp.where((first_expert == own) & (first >= 0), first, placement)
    slots = lax.broadcasted_iota(jnp.int32, (PADDED, placement.shape[1]), 0)
    hot = (slots == placement).astype(jnp.bfloat16)
    for load in loads[len(ids) :]:
        load.wait()
    rows = jnp.dot(hot, block_ref[...], preferred_element_type=jnp.float32).astype(jnp.bfloat16)
    for i in range(out_ref.shape[0]):
        out_ref[i] = rows[:SLOTS]


def products_kernel(rows_ref, own_ref, gate_other_ref, up_other_ref, out_ref):
    rows = rows_ref[...]
    units = gate_other_ref.shape[1]

    def product(at, w):
        out_ref[:, at * units : (at + 1) * units] = jnp.dot(
            rows, w, preferred_element_type=jnp.float32
        ).astype(jnp.bfloat16)

    product(0, own_ref[:, :units])
    product(1, gate_other_ref[...])
    product(2, own_ref[:, units:])
    product(3, up_other_ref[...])


def hidden_kernel(parts_ref, out_ref):
    units = out_ref.shape[2]
    total = parts_ref[0].astype(jnp.float32)
    for i in range(1, parts_ref.shape[0]):
        total += parts_ref[i].astype(jnp.float32)
    gate, up = total[:, :units], total[:, units:]
    hidden = (gate / (1.0 + jnp.exp(-gate)) * up).astype(jnp.bfloat16)
    for i in range(out_ref.shape[0]):
        out_ref[i] = hidden


def total_kernel(parts_ref, out_ref):
    total = parts_ref[0].astype(jnp.float32)
    for i in range(1, parts_ref.shape[0]):
        total += parts_ref[i].astype(jnp.float32)
    rows = jnp.concatenate([total, jnp.zeros((PADDED - SLOTS, total.shape[1]), jnp.float32)], axis=0)
    rows = rows.astype(jnp.bfloat16)
    for i in range(out_ref.shape[0]):
        out_ref[i] = rows


def finish_kernel(
    tokens_ref, table_ref, column_ref, gate_ref, gain_ref, w_hbm, mixed_ref, query_ref, normed_ref, w_ref, sem
):
    parts = w_ref.shape[0]
    loads = [pltpu.make_async_copy(w_hbm.at[i], w_ref.at[i], sem.at[i]) for i in range(parts)]
    for load in loads:
        load.start()
    blocks = table_ref.shape[0] // (2 * PADDED)
    tok_count, width = tokens_ref.shape
    block_width = width // blocks
    column = column_ref[...]
    slots = lax.broadcasted_iota(jnp.int32, (tok_count, PADDED), 1)
    hot = [(column == slots + e * PADDED).astype(jnp.bfloat16) for e in range(2)]
    gate = gate_ref[...]
    square = jnp.zeros((tok_count, LANES), jnp.float32)
    for z in range(blocks):
        cols = pl.ds(z * block_width, block_width)
        picked = sum(
            jnp.dot(
                hot[e],
                table_ref[pl.ds((e * blocks + z) * PADDED, PADDED), :],
                preferred_element_type=jnp.float32,
            )
            for e in range(2)
        )
        mixed = (tokens_ref[:, cols].astype(jnp.float32) + gate * picked).astype(jnp.bfloat16)
        mixed_ref[:, cols] = mixed
        values = mixed.astype(jnp.float32)
        for i in range(block_width // LANES):
            part = values[:, i * LANES : (i + 1) * LANES]
            square += part * part
    mean = jnp.sum(square, axis=1, keepdims=True) * (1.0 / width)
    scale = lax.rsqrt(mean + 1e-05)
    for z in range(blocks):
        cols = pl.ds(z * block_width, block_width)
        values = mixed_ref[:, cols].astype(jnp.float32)
        normed_ref[:, cols] = (values * scale * gain_ref[:, cols]).astype(jnp.bfloat16)
    cores, ys, rows = w_ref.shape[1:4]
    pair = 2 * cores * rows
    query = jnp.zeros(query_ref.shape, jnp.float32)
    for x in range(0, parts, 2):
        loads[x].wait()
        loads[x + 1].wait()
        for y in range(ys):
            block = jnp.concatenate([w_ref[x + i, c, y] for i in range(2) for c in range(cores)], axis=0)
            start = (y * parts + x) * cores * rows
            query += jnp.dot(
                normed_ref[:, start : start + pair], block, preferred_element_type=jnp.float32
            )
    query_ref[...] = query.astype(query_ref.dtype)


def finish(tokens, table, column, gate, gain, w_query):
    vmem = pl.BlockSpec(memory_space=pltpu.VMEM)
    tok_count, width = tokens.shape
    columns = w_query.shape[-1]
    return pl.pallas_call(
        finish_kernel,
        out_shape=(
            jax.ShapeDtypeStruct((tok_count, width), jnp.bfloat16),
            jax.ShapeDtypeStruct((tok_count, columns), jnp.bfloat16),
        ),
        in_specs=[vmem] * 5 + [pl.BlockSpec(memory_space=pltpu.HBM)],
        out_specs=(vmem, vmem),
        scratch_shapes=[
            pltpu.VMEM((tok_count, width), jnp.bfloat16),
            pltpu.VMEM(w_query.shape, jnp.bfloat16),
            pltpu.SemaphoreType.DMA((w_query.shape[0],)),
        ],
        compiler_params=pltpu.CompilerParams(vmem_limit_bytes=FINISH_BYTES),
        cost_estimate=pl.CostEstimate(
            flops=2 * tok_count * width * columns, bytes_accessed=4 * width * columns, transcendentals=0
        ),
    )(tokens, table, column[:, None], gate[:, None], gain[None, :], w_query)


def local(
    tokens,
    first_expert,
    first_slot,
    second_expert,
    second_slot,
    first_gate,
    second_gate,
    w_gate,
    w_up,
    w_down,
    norm_gain,
    w_query,
):
    tok_count, width = tokens.shape
    blocks = lax.axis_size("z")
    chips = lax.axis_size(CHIPS)
    block_width = width // blocks
    units = w_gate.shape[1]
    experts = lax.axis_size("y_lo")

    served_first = first_slot >= 0
    served = served_first | (second_slot >= 0)
    expert_of = jnp.where(served_first, first_expert, second_expert)
    slot_of = jnp.where(served_first, first_slot, second_slot + CAP1)
    gate_of = jnp.where(served_first, first_gate, second_gate)

    slot_copies = small_call(
        slots_kernel,
        (chips, SLOTS, block_width),
        0,
        tokens,
        first_expert[None, :],
        first_slot[None, :],
        second_expert[None, :],
        second_slot[None, :],
        scratch=(
            pltpu.VMEM((tok_count, block_width), jnp.bfloat16),
            *[pltpu.VMEM((1, tok_count), jnp.int32)] * 4,
            pltpu.SemaphoreType.DMA((4 + PIECES,)),
        ),
    )
    slot_copies, w_query = tie(slot_copies, w_query)
    rows = exchange(slot_copies, CHIPS).reshape(chips * SLOTS, block_width)
    w_gate_other = other_core(w_gate)
    w_up_other = other_core(w_up)
    w_query_beside = across(w_query, 1)

    w_own = jnp.concatenate([w_gate, w_up], axis=1)
    partial = small_call(
        products_kernel, (chips * SLOTS, 4 * units), 4, rows, w_own, w_gate_other, w_up_other
    )
    share = chips * SLOTS // blocks
    partial, w_query, w_query_beside = tie(partial, w_query, w_query_beside)
    summed = exchange(partial.reshape(blocks, share, 4 * units), "z")
    query_rows = in_order(w_query, w_query_beside, 1, 0)
    query_rows_other = across(query_rows, 2)
    hidden_copies = small_call(hidden_kernel, (blocks, share, 2 * units), 1, summed)
    hidden_copies, query_rows_other = tie(hidden_copies, query_rows_other)
    query_rows = in_order(query_rows, query_rows_other, 2, 0).reshape((-1,) + w_query.shape)
    w_query_full = lax.all_gather(query_rows, ("x", "core"), axis=0)
    w_query_full = w_query_full.reshape((-1, 2) + query_rows.shape)
    hidden = exchange(hidden_copies, "z").reshape(chips * SLOTS, 2 * units)
    w_down_other = other_core(w_down)
    out_part = jnp.dot(hidden[:, :units], w_down, preferred_element_type=jnp.float32) + jnp.dot(
        hidden[:, units:], w_down_other, preferred_element_type=jnp.float32
    )
    out_part = out_part.astype(jnp.bfloat16)
    pieces = exchange(out_part.reshape(chips, SLOTS, block_width), CHIPS)
    out_copies = small_call(total_kernel, (experts * blocks, PADDED, block_width), 1, pieces)
    table = exchange(out_copies, EXPERT).reshape(-1, block_width)

    column = jnp.where(served, expert_of * PADDED + slot_of, -1)
    return finish(tokens, table, column, gate_of, norm_gain, w_query_full)


def solution(mesh):
    fine = Mesh(mesh.devices.reshape(tuple(SIZES.values())), tuple(SIZES))
    in_specs = (
        P(DP, None),
        P(DP),
        P(DP),
        P(DP),
        P(DP),
        P(DP),
        P(DP),
        P(EXPERT, DP),
        P(EXPERT, DP),
        P(DP, EXPERT),
        P(),
        P(DP, EXPERT),
    )
    out_specs = (P(DP, None), P(DP, EXPERT))
    return jax.shard_map(local, mesh=fine, in_specs=in_specs, out_specs=out_specs, check_vma=False)
```
